32 devices in a mesh: cases: 2 (over y), gx: 4 (over z), gy: 2 (over x), gz: 2 (over core).
Axes of the slice: x: 2, y: 2, z: 4, core: 2. Of those that a mesh axis runs over, the one named last changes fastest.
Arguments:
- adjoint_state: float32 [26, 128, 16, 256], P(None, ('cases', 'gx'), 'gy', 'gz'), parts along dimension 1, may hold values from -6 to 6
- macroscopic_state: float32 [5, 128, 16, 256], P(None, ('cases', 'gx'), 'gy', 'gz'), parts along dimension 1, may hold values from -0.3 to 2, as said below
- design: float32 [128, 16, 256], P(('cases', 'gx'), 'gy', 'gz'), parts along dimension 0, may hold values from 0.05 to 1
- solid: int32 [128, 16, 256], P(('cases', 'gx'), 'gy', 'gz'), parts along dimension 0, may hold values 0 or 1
- heated: int32 [128, 16], P(('cases', 'gx'), 'gy'), parts along dimension 0, may hold values 0 or 1
- face_labels: int32 [4, 16, 256], P('cases', 'gy', 'gz'), parts along dimension 0, may hold values from 0 to 1
- radius: int32 [128], P('cases'), parts along dimension 0, may hold values from 1 to 2, as said below
Outputs:
- adjoint_next: float32 [26, 128, 16, 256], P(None, ('cases', 'gx'), 'gy', 'gz'), parts along dimension 1
- sensitivity: float32 [128, 16, 256], P(('cases', 'gx'), 'gy', 'gz'), parts along dimension 0
The draws below stay inside these ranges and needn't reach their ends.
There are 2 independent parts, one for each index of `cases`. The reference program is written for one: setup_inputs(seed, part) draws one part's arguments, and reference() takes and returns one part's arrays. A program takes and returns all parts, laid end to end along the dimension named above; each array names one. Nothing has to cross between parts.
Inputs may be any that keep to these rules, and one draw needn't show every extreme that they name: `macroscopic_state`: component 0 is a positive density, 1 to 3 a velocity, 4 a temperature. `face_labels`: 0 is a closed wall cell of the face, 1 an open one. `radius`: both radii 1 and 2 occur.
All inputs are finite; a program needn't handle non-finite values. No bound on the sum of `solid` or of `heated` on one device may be relied on, other than what follows from the above.
Results may differ from the reference program's by a relative error of at most 0.000088.
Values sent between devices are 32-bit elements; how exact they have to be, the bound alone decides.
A program may use at most 64 MiB of HBM per device.

```python
import jax
import jax.numpy as jnp
import numpy as np
from jax import lax

LATTICE_SPAN_Z = 256
LATTICE_SPAN_X = 64
LATTICE_SPAN_Y = 16


def draw_macroscopic_state(key, part):
    key = jax.random.fold_in(key, 11)
    first, second, smoothing_final_pass = jax.random.split(key, 3)
    mass_per_site = jax.random.uniform(first, (1, LATTICE_SPAN_X, LATTICE_SPAN_Y, LATTICE_SPAN_Z), jnp.float32, 0.8, 1.2)
    flow_speeds = jnp.clip(0.12 * jax.random.normal(second, (3, LATTICE_SPAN_X, LATTICE_SPAN_Y, LATTICE_SPAN_Z), jnp.float32), -0.3, 0.3)
    thermal_values = jax.random.uniform(smoothing_final_pass, (1, LATTICE_SPAN_X, LATTICE_SPAN_Y, LATTICE_SPAN_Z), jnp.float32, 0.2, 1.5)
    return jnp.concatenate([mass_per_site, flow_speeds, thermal_values])


def draw_radius(key, part):
    key = jax.random.fold_in(key, 23)
    first, second, smoothing_final_pass = jax.random.split(key, 3)
    values = jax.random.randint(first, (LATTICE_SPAN_X,), 1, 3)
    spot = jax.random.randint(second, (), 0, LATTICE_SPAN_X)
    other = (spot + 1 + jax.random.randint(smoothing_final_pass, (), 0, LATTICE_SPAN_X - 1)) % LATTICE_SPAN_X
    places = jnp.arange(LATTICE_SPAN_X, dtype=jnp.int32)
    values = jnp.where(places == spot, 2, values)
    values = jnp.where(places == other, 1, values)
    return values.astype(jnp.int32)


def touch_ends(drawn, key, least, top_value):
    spot = [jax.random.randint(jax.random.fold_in(key, axis), (), 0, length) for axis, length in enumerate(drawn.shape)]
    longest = drawn.shape.index(max(drawn.shape))
    beside = spot[:longest] + [(spot[longest] + 1) % drawn.shape[longest]] + spot[longest + 1:]
    return drawn.at[tuple(spot)].set(least).at[tuple(beside)].set(top_value)


def level_of(key, shape, pieces, least, high):
    factor_of, own = 1.0, jax.random.fold_in(key, 6)
    for position, parts in pieces:
        draws = jnp.exp(jax.random.uniform(jax.random.fold_in(own, position), (parts,), jnp.float32, least / len(pieces), high / len(pieces)))
        factor_of = factor_of * jnp.repeat(draws, shape[position] // parts).reshape([-1 if axis == position else 1 for axis in range(len(shape))])
    return factor_of


def gaussian(rng, extent, deviation, bound, cuts=(), kind=jnp.bfloat16):
    loudness = level_of(rng, extent, cuts, -0.22, 0.18) if cuts else 1.0
    drawn = jax.random.normal(rng, extent, jnp.float32) * deviation * loudness
    return jnp.minimum(jnp.maximum(drawn, -bound), bound).astype(kind)


def setup_inputs(seed: int = 0, part: int = 0) -> dict:
    key_of = jax.random.split(jax.random.key(seed), 8)
    part_keys = jax.random.split(jax.random.fold_in(key_of[7], part), 8)
    adjoint_state = gaussian(part_keys[0], (26, LATTICE_SPAN_X, LATTICE_SPAN_Y, LATTICE_SPAN_Z), 1.0, 6.0, ((1, 4), (2, 2), (3, 2)), jnp.float32)
    macroscopic_state = draw_macroscopic_state(jax.random.fold_in(jax.random.fold_in(key_of[7], part), 71), part)
    design = jnp.clip(0.05 + 0.95 * jax.random.uniform(part_keys[2], (LATTICE_SPAN_X, LATTICE_SPAN_Y, LATTICE_SPAN_Z), jnp.float32) ** level_of(part_keys[2], (LATTICE_SPAN_X, LATTICE_SPAN_Y, LATTICE_SPAN_Z), ((0, 4), (1, 2), (2, 2)), -0.2, 0.2), 0.05, 1.0)
    solid = touch_ends((jax.random.randint(part_keys[3], (LATTICE_SPAN_X, LATTICE_SPAN_Y, LATTICE_SPAN_Z), 0, 8) < 1).astype(jnp.int32), jax.random.fold_in(part_keys[3], 1), 0, 1)
    heated = touch_ends((jax.random.randint(part_keys[4], (LATTICE_SPAN_X, LATTICE_SPAN_Y), 0, 2) < 1).astype(jnp.int32), jax.random.fold_in(part_keys[4], 1), 0, 1)
    face_labels = touch_ends(jax.random.randint(part_keys[5], (2, LATTICE_SPAN_Y, LATTICE_SPAN_Z), 0, 2), jax.random.fold_in(part_keys[5], 1), 0, 1).astype(jnp.int32)
    radius = draw_radius(jax.random.fold_in(jax.random.fold_in(key_of[7], part), 71), part)
    return dict(adjoint_state=adjoint_state, macroscopic_state=macroscopic_state, design=design, solid=solid, heated=heated, face_labels=face_labels, radius=radius)


FLOW_VECTORS = [(0, 0, 0), (1, 0, 0), (-1, 0, 0), (0, 1, 0), (0, -1, 0), (0, 0, 1), (0, 0, -1),
                (1, 1, 0), (-1, -1, 0), (1, -1, 0), (-1, 1, 0), (1, 0, 1), (-1, 0, -1),
                (1, 0, -1), (-1, 0, 1), (0, 1, 1), (0, -1, -1), (0, 1, -1), (0, -1, 1)]
DIRECTIONS = [(0, 0, 0), (1, 0, 0), (-1, 0, 0), (0, 1, 0), (0, -1, 0), (0, 0, 1), (0, 0, -1),
              (1, 1, 0), (-1, -1, 0), (1, -1, 0), (-1, 1, 0), (1, 0, 1), (-1, 0, -1),
              (1, 0, -1), (-1, 0, 1), (0, 1, 1), (0, -1, -1), (0, 1, -1), (0, -1, 1),
              (0, 0, 0), (1, 0, 0), (-1, 0, 0), (0, 1, 0), (0, -1, 0), (0, 0, 1), (0, 0, -1)]
FLOW_OPPOSITE = [0, 2, 1, 4, 3, 6, 5, 8, 7, 10, 9, 12, 11, 14, 13, 16, 15, 18, 17]
OPPOSITE = [0, 2, 1, 4, 3, 6, 5, 8, 7, 10, 9, 12, 11, 14, 13, 16, 15, 18, 17,
            19, 21, 20, 23, 22, 25, 24]
RELAX_FLOW = 1.6
THERMAL_OMEGA = 1.25
WALL_WEIGHT = 0.5
MOMENT_PATTERNS = [(), (0,), (1,), (2,), (0, 0), (1, 1), (2, 2), (0, 1), (0, 2), (1, 2)]


def moment_table(weights, vectors):
    rows = []
    for pattern in MOMENT_PATTERNS:
        entries = []
        for weight, vector in zip(weights, vectors):
            value = float(weight)
            for place in pattern:
                value = value * float(vector[place])
            entries.append(value)
        rows.append(entries)
    return np.array(rows, dtype=np.float32)


def build_tables():
    flow_moments = moment_table([1.0 / 3.0] + [1.0 / 18.0] * 6 + [1.0 / 36.0] * 12, FLOW_VECTORS)
    heat_moments = moment_table([0.25] + [0.125] * 6, FLOW_VECTORS[:7])[:4]
    flow_basis = np.array([[1.0] + [float(entry) for entry in vector] for vector in FLOW_VECTORS], dtype=np.float32)
    return flow_moments, heat_moments, flow_basis


def shifted_views(padded, length_x, length_y, length_z):
    views = []
    for member in range(26):
        vector = DIRECTIONS[member]
        views.append(padded[member, 1 + vector[0]:1 + vector[0] + length_x,
                            1 + vector[1]:1 + vector[1] + length_y, 1 + vector[2]:1 + vector[2] + length_z])
    return views


def reduce_or(flags):
    total = flags[0]
    for other in flags[1:]:
        total = total | other
    return total


def settle(moved, local, coord_x, coord_y, coord_z, full_x, full_y, full_z, labels):
    result = []
    for member in range(26):
        vector = DIRECTIONS[member]
        value = moved[member]
        if vector == (0, 0, 0):
            result.append(value)
            continue
        flags = []
        out_x = None
        if vector[0] != 0:
            out_x = (coord_x + vector[0] < 0) | (coord_x + vector[0] >= full_x)
            flags.append(out_x)
        if vector[1] != 0:
            flags.append((coord_y + vector[1] < 0) | (coord_y + vector[1] >= full_y))
        if vector[2] != 0:
            flags.append((coord_z + vector[2] < 0) | (coord_z + vector[2] >= full_z))
        outside = reduce_or(flags)
        bounce = local[OPPOSITE[member]]
        if out_x is not None:
            face = labels[0] if vector[0] < 0 else labels[1]
            opened = out_x & (face == 1)[None]
            for other in flags[1:]:
                opened = opened & jnp.logical_not(other)
            bounce = jnp.where(opened, jnp.zeros_like(bounce), bounce)
        result.append(jnp.where(outside, bounce, value))
    return jnp.stack(result)


def collide(pulled, macroscopic_state, design, solid, source):
    highest = lax.Precision.HIGHEST
    flow_moments, heat_moments, flow_basis = build_tables()
    flow = pulled[:19]
    heat = pulled[19:]
    flow_sums = jnp.einsum('mi,ixyz->mxyz', jnp.asarray(flow_moments).astype(flow.dtype), flow, precision=highest)
    heat_sums = jnp.einsum('mi,ixyz->mxyz', jnp.asarray(heat_moments).astype(flow.dtype), heat, precision=highest)
    mass_per_site = macroscopic_state[0]
    vel_x = macroscopic_state[1]
    vel_y = macroscopic_state[2]
    vel_z = macroscopic_state[3]
    thermal_values = macroscopic_state[4]
    fluid = jnp.where(solid == 1, 0.0, 1.0).astype(flow.dtype)
    fluid_site_mask = design * fluid
    squared = fluid_site_mask * fluid_site_mask
    zeroth = flow_sums[0]
    tensor_x = flow_sums[4] * vel_x + flow_sums[7] * vel_y + flow_sums[8] * vel_z
    tensor_y = flow_sums[7] * vel_x + flow_sums[5] * vel_y + flow_sums[9] * vel_z
    tensor_z = flow_sums[8] * vel_x + flow_sums[9] * vel_y + flow_sums[6] * vel_z
    quad = vel_x * tensor_x + vel_y * tensor_y + vel_z * tensor_z
    speed_sq = vel_x * vel_x + vel_y * vel_y + vel_z * vel_z
    first_u = flow_sums[1] * vel_x + flow_sums[2] * vel_y + flow_sums[3] * vel_z
    thermal_advection = heat_sums[1] * vel_x + heat_sums[2] * vel_y + heat_sums[3] * vel_z
    buoyant_exchange = THERMAL_OMEGA * 4.0 * fluid_site_mask * thermal_values / mass_per_site
    d_rho = RELAX_FLOW * (zeroth - squared * (4.5 * quad - 1.5 * speed_sq * zeroth)) - buoyant_exchange * thermal_advection
    d_mx = RELAX_FLOW * (3.0 * fluid_site_mask * flow_sums[1] + squared * (9.0 * tensor_x - 3.0 * zeroth * vel_x)) + buoyant_exchange * heat_sums[1]
    d_my = RELAX_FLOW * (3.0 * fluid_site_mask * flow_sums[2] + squared * (9.0 * tensor_y - 3.0 * zeroth * vel_y)) + buoyant_exchange * heat_sums[2]
    d_mz = RELAX_FLOW * (3.0 * fluid_site_mask * flow_sums[3] + squared * (9.0 * tensor_z - 3.0 * zeroth * vel_z)) + buoyant_exchange * heat_sums[3]
    gradient = jnp.stack([d_rho, d_mx, d_my, d_mz])
    collided = (1.0 - RELAX_FLOW) * flow + jnp.einsum('ic,cxyz->ixyz', jnp.asarray(flow_basis).astype(flow.dtype), gradient, precision=highest)
    bounced = jnp.stack([flow[other] for other in FLOW_OPPOSITE])
    flow_next = jnp.where(solid[None] == 1, bounced, collided)
    heat_next = (1.0 - THERMAL_OMEGA) * heat + (THERMAL_OMEGA * (heat_sums[0] + 4.0 * fluid_site_mask * thermal_advection) + WALL_WEIGHT * source)[None]
    term = fluid * (RELAX_FLOW * mass_per_site * (3.0 * first_u + fluid_site_mask * (9.0 * quad - 3.0 * speed_sq * zeroth))
                    + THERMAL_OMEGA * 4.0 * thermal_values * thermal_advection)
    return jnp.concatenate([flow_next, heat_next]), term


def split_by_radius(term, radius_here):
    reach = radius_here.reshape(-1, 1, 1)
    volume = ((2 * reach + 1) ** 3).astype(term.dtype)
    scaled = term / volume
    return jnp.stack([jnp.where(reach == 1, scaled, jnp.zeros_like(scaled)),
                      jnp.where(reach == 2, scaled, jnp.zeros_like(scaled))])


def window(values, axis, reach, length):
    total = lax.slice_in_dim(values, 2 - reach, 2 - reach + length, axis=axis)
    for offset in range(1 - reach, reach + 1):
        total = total + lax.slice_in_dim(values, 2 + offset, 2 + offset + length, axis=axis)
    return total


def box_sum(rimmed, length_x, length_y, length_z):
    total = None
    for member in range(2):
        reach = member + 1
        values = window(rimmed[member], 0, reach, length_x)
        values = window(values, 1, reach, length_y)
        values = window(values, 2, reach, length_z)
        total = values if total is None else total + values
    return total


def reference(adjoint_state, macroscopic_state, design, solid, heated, face_labels, radius):
    coord_x = jnp.arange(LATTICE_SPAN_X, dtype=jnp.int32).reshape(LATTICE_SPAN_X, 1, 1)
    coord_y = jnp.arange(LATTICE_SPAN_Y, dtype=jnp.int32).reshape(1, LATTICE_SPAN_Y, 1)
    coord_z = jnp.arange(LATTICE_SPAN_Z, dtype=jnp.int32).reshape(1, 1, LATTICE_SPAN_Z)
    padded = jnp.pad(adjoint_state, ((0, 0), (1, 1), (1, 1), (1, 1)))
    moved = shifted_views(padded, LATTICE_SPAN_X, LATTICE_SPAN_Y, LATTICE_SPAN_Z)
    pulled = settle(moved, adjoint_state, coord_x, coord_y, coord_z, LATTICE_SPAN_X, LATTICE_SPAN_Y, LATTICE_SPAN_Z, face_labels)
    source = jnp.where((coord_z == 0) & (heated[:, :, None] == 1), 1.0, 0.0).astype(adjoint_state.dtype)
    adjoint_next, term = collide(pulled, macroscopic_state, design, solid, source)
    pair = split_by_radius(term, radius)
    rimmed = jnp.pad(pair, ((0, 0), (2, 2), (2, 2), (2, 2)))
    sensitivity = box_sum(rimmed, LATTICE_SPAN_X, LATTICE_SPAN_Y, LATTICE_SPAN_Z)
    return adjoint_next, sensitivity
```

```python
import jax
import jax.numpy as jnp
from jax import lax
from jax.experimental import pallas as pl
from jax.experimental.pallas import tpu as pltpu
from jax.sharding import PartitionSpec as P

VECTORS = [
    (0, 0, 0),
    (1, 0, 0), (-1, 0, 0), (0, 1, 0), (0, -1, 0), (0, 0, 1), (0, 0, -1),
    (1, 1, 0), (-1, -1, 0), (1, -1, 0), (-1, 1, 0),
    (1, 0, 1), (-1, 0, -1), (1, 0, -1), (-1, 0, 1),
    (0, 1, 1), (0, -1, -1), (0, 1, -1), (0, -1, 1),
]
VECTORS = VECTORS + VECTORS[:7]
OPP = [0, 2, 1, 4, 3, 6, 5, 8, 7, 10, 9, 12, 11, 14, 13, 16, 15, 18, 17, 19, 21, 20, 23, 22, 25, 24]
X_FROM = ([2, 8, 10, 12, 14, 21], [1, 7, 9, 11, 13, 20])
Y_FROM = ([4, 8, 9, 16, 18, 23], [3, 7, 10, 15, 17, 22])
Z_PAIRS = [(5, 6, 0), (15, 17, 16), (18, 16, 32), (24, 25, 48), (11, 13, 64), (14, 12, 96)]
Z_BASE = {i: base for a, b, base in Z_PAIRS for i in (a, b)}
MESH = pl.DeviceIdType.MESH
W0, W1, W2 = 1.0 / 3.0, 1.0 / 18.0, 1.0 / 36.0

ROUND_1 = (
    [(dx, 0, 0) for dx in (1, -1)]
    + [(0, dy, 0) for dy in (1, -1)]
    + [(0, 0, 1)]
    + [(dx, dy, 0) for dx in (1, -1) for dy in (1, -1)]
    + [(dx, 0, 1) for dx in (1, -1)]
    + [(0, dy, 1) for dy in (1, -1)]
)
ROUND_2 = ROUND_1 + [(dx, dy, 1) for dx in (1, -1) for dy in (1, -1)]


def kernel(
    nx, state, macro, design, solid, heated, faces, radius, out, sens,
    S, MA, DE, SO, HE, FA, O, G, xs, xr, ys, yh, zs, zh, xzr, yzr,
    tp, tys, trow, tyz, tzs, tz, zr, Wb, hT, SE,
    in_sem, out_sem, send1, recv1, send2, recv2,
):
    f32 = jnp.float32
    px, py = lax.axis_size("gx"), lax.axis_size("gy")
    me_c, me_x = lax.axis_index("cases"), lax.axis_index("gx")
    me_y, me_z = lax.axis_index("gy"), lax.axis_index("gz")

    def has(d):
        flag = None
        for delta, me, count in ((d[0], me_x, px), (d[1], me_y, py)):
            if delta == 0:
                continue
            here = me < count - 1 if delta > 0 else me > 0
            flag = here if flag is None else jnp.logical_and(flag, here)
        return flag

    def when(flag, body):
        if flag is None:
            body()
        else:
            pl.when(flag)(body)

    def target(d):
        return (me_c, me_x + d[0], me_y + d[1], 1 - me_z if d[2] else me_z)

    loads = [
        pltpu.make_async_copy(state, S.at[:, 1 : 1 + nx], in_sem.at[0]),
        pltpu.make_async_copy(macro, MA, in_sem.at[1]),
        pltpu.make_async_copy(design, DE, in_sem.at[2]),
        pltpu.make_async_copy(solid, SO, in_sem.at[3]),
        pltpu.make_async_copy(heated, HE, in_sem.at[4]),
        pltpu.make_async_copy(faces, FA, in_sem.at[5]),
    ]
    for load in loads:
        load.start()

    trow[...] = jnp.zeros_like(trow)
    tyz[...] = jnp.zeros_like(tyz)
    tz[...] = jnp.zeros_like(tz)
    tp[0:2] = jnp.zeros((2, 8, 128), f32)
    tp[nx + 2 : nx + 4] = jnp.zeros((2, 8, 128), f32)

    barrier = pltpu.get_barrier_semaphore()
    for d in ROUND_2:
        def greet(d=d):
            pl.semaphore_signal(barrier, inc=1, device_id=target(d), device_id_type=MESH)
        when(has(d), greet)

    lane = lax.broadcasted_iota(jnp.int32, (8, 128), 1)
    sub = lax.broadcasted_iota(jnp.int32, (8, 128), 0)
    edge = 127 * me_z
    mine = 127 - edge

    for load in loads:
        load.wait()

    for side, (x_at, y_at) in enumerate(((nx, 7), (1, 0))):
        for j in range(6):
            xs[side, j] = S[X_FROM[side][j], x_at]
            ys[side, j] = S[Y_FROM[side][j], 1 : 1 + nx, y_at, :]

    def pack(x, acc):
        for first, second, base in Z_PAIRS:
            v = S[jnp.where(me_z == 1, first, second), x + 1]
            moved = pltpu.roll(v, lax.rem(base + x - mine + 256, 128), 1)
            acc = jnp.where(lane == base + x, moved, acc)
        return acc

    zs[...] = lax.fori_loop(0, nx, pack, jnp.zeros((8, 128), f32), unroll=True)

    beside_x = jnp.where(me_x > 0, 1, 0) + jnp.where(me_x < px - 1, 1, 0)
    beside_y = jnp.where(me_y > 0, 1, 0) + jnp.where(me_y < py - 1, 1, 0)
    pl.semaphore_wait(barrier, 2 * (beside_x + 1) * (beside_y + 1) - 1)

    def refs_1(d):
        dx, dy, dz = d
        side_x, side_y = (0 if dx > 0 else 1), (0 if dy > 0 else 1)
        if dx and dy:
            j = next(k for k, i in enumerate(Y_FROM[side_y]) if VECTORS[i][0] == -dx)
            if dx > 0:
                return ys.at[side_y, j, nx - 8 : nx], yh.at[side_y, j, 0:8]
            return ys.at[side_y, j, 0:8], yh.at[side_y, j, nx + 8 : nx + 16]
        if dx and dz:
            pair = (14, 12) if dx > 0 else (11, 13)
            return S.at[jnp.where(me_z == 1, pair[0], pair[1]), nx if dx > 0 else 1], xzr.at[side_x]
        if dy and dz:
            j = jnp.where(me_z == 1, 4, 3) if dy > 0 else jnp.where(me_z == 1, 3, 4)
            return ys.at[side_y, j], yzr.at[side_y]
        if dx:
            return xs.at[side_x], xr.at[side_x]
        if dy:
            return ys.at[side_y], yh.at[side_y, :, 8 : 8 + nx]
        return zs, zh

    def refs_2(d):
        dx, dy, dz = d
        side_y = 0 if dy > 0 else 1
        if dy:
            into = tyz if dz else trow
            if dx > 0:
                return tys.at[side_y, :, nx - 8 : nx], into.at[side_y, :, 0:8]
            if dx < 0:
                return tys.at[side_y, :, 0:8], into.at[side_y, :, nx + 8 : nx + 16]
            return tys.at[side_y], into.at[side_y, :, 8 : 8 + nx]
        if dz:
            return tzs, tz.at[0 if dx == 0 else 1 if dx > 0 else 2]
        if dx > 0:
            return tp.at[nx : nx + 2], tp.at[0:2]
        return tp.at[2:4], tp.at[nx + 2 : nx + 4]

    def copies(messages, refs, sends, recvs):
        made = []
        for n, d in enumerate(messages):
            src, dst = refs(d)
            made.append(
                pltpu.make_async_remote_copy(
                    src_ref=src, dst_ref=dst, send_sem=sends.at[n], recv_sem=recvs.at[n],
                    device_id=target(d), device_id_type=MESH,
                )
            )
        return made

    def start(messages, made):
        for d, copy in zip(messages, made):
            when(has(d), copy.start)

    def arrive(messages, made):
        for d, copy in zip(messages, made):
            when(has((-d[0], -d[1], d[2])), copy.wait_recv)

    def leave(messages, made):
        for d, copy in zip(messages, made):
            when(has(d), copy.wait_send)

    round_1 = copies(ROUND_1, refs_1, send1, recv1)
    start(ROUND_1, round_1)

    hT[...] = jnp.zeros_like(hT)
    hT[:, 0:nx] = jnp.where(HE[...] == 1, 1.0, 0.0)

    core = jnp.full((8, 128), me_z, jnp.int32)
    col_p = (lane == 0) & (core == 0)
    col_m = (lane == 127) & (core == 1)
    out_z = {1: (lane == 127) & (core == 1), -1: (lane == 0) & (core == 0)}
    at_y = jnp.full((8, 128), me_y, jnp.int32)
    out_y = {1: (sub == 7) & (at_y == py - 1), -1: (sub == 0) & (at_y == 0)}
    face = {1: FA[1] == 1, -1: FA[0] == 1}
    heat_lane = (lane == 0) & (core == 0)

    arrive(ROUND_1, round_1)

    for side, at in ((0, 0), (1, nx + 1)):
        for j in range(6):
            S[X_FROM[side][j], at] = xr[side, j]
    lane_r = lax.broadcasted_iota(jnp.int32, (nx, 128), 1)
    core_r = jnp.full((nx, 128), me_z, jnp.int32)
    for side in (0, 1):
        for j in (3, 4):
            up = VECTORS[Y_FROM[side][j]][2] > 0
            mask = (lane_r == (0 if up else 127)) & (core_r == (0 if up else 1))
            yh[side, j, 8 : 8 + nx] = jnp.where(mask, yzr[side], yh[side, j, 8 : 8 + nx])
    cols = zh[...]
    cols = jnp.where(lane == 80, pltpu.roll(xzr[1], lax.rem(80 - edge + 128, 128), 1), cols)
    cols = jnp.where(lane == 95, pltpu.roll(xzr[0], lax.rem(95 - edge + 128, 128), 1), cols)
    zh[...] = cols

    first_slab = me_x * nx

    def slab_a(x, carry):
        cols = zh[...]
        at_x = jnp.full((8, 128), first_slab + x, jnp.int32)
        out_x = {1: at_x == px * nx - 1, -1: at_x == 0}
        column = {}
        for first, second, base in Z_PAIRS:
            k = base + x + VECTORS[first][0]
            column[base] = pltpu.roll(cols, lax.rem(edge - k + 256, 128), 1)
        g = []
        for i in range(26):
            cx, cy, cz = VECTORS[i]
            v = S[i, x + 1 + cx]
            if cz:
                v = jnp.where(col_p if cz > 0 else col_m, column[Z_BASE[i]], v)
            if cy:
                side = 0 if cy < 0 else 1
                row = yh[side, Y_FROM[side].index(i), pl.ds(8 + x + cx, 1), :]
                v = jnp.where(sub == (0 if cy > 0 else 7), row, v)
                v = pltpu.roll(v, 7 if cy > 0 else 1, 0)
            if cz:
                v = pltpu.roll(v, 127 if cz > 0 else 1, 1)
            if (cx, cy, cz) != (0, 0, 0):
                bounce = S[OPP[i], x + 1]
                leaves = None
                if cy:
                    leaves = out_y[cy]
                if cz:
                    leaves = out_z[cz] if leaves is None else leaves | out_z[cz]
                if cx:
                    opened = out_x[cx] & face[cx]
                    if leaves is not None:
                        opened = opened & jnp.logical_not(leaves)
                    bounce = jnp.where(opened, 0.0, bounce)
                    leaves = out_x[cx] if leaves is None else leaves | out_x[cx]
                v = jnp.where(leaves, bounce, v)
            O[i, x] = v
            g.append(v)
        s = {i: g[i] + g[i + 1] for i in range(1, 19, 2)}
        d = {i: g[i] - g[i + 1] for i in range(1, 19, 2)}
        xy, xz, yz = s[7] + s[9], s[11] + s[13], s[15] + s[17]
        g0 = W0 * g[0] + W1 * (s[1] + s[3] + s[5]) + W2 * (xy + xz + yz)
        g1x = W1 * d[1] + W2 * ((d[7] + d[9]) + (d[11] + d[13]))
        g1y = W1 * d[3] + W2 * ((d[7] - d[9]) + (d[15] + d[17]))
        g1z = W1 * d[5] + W2 * ((d[11] - d[13]) + (d[15] - d[17]))
        gxx = W1 * s[1] + W2 * (xy + xz)
        gyy = W1 * s[3] + W2 * (xy + yz)
        gzz = W1 * s[5] + W2 * (xz + yz)
        gxy, gxz, gyz = W2 * (s[7] - s[9]), W2 * (s[11] - s[13]), W2 * (s[15] - s[17])
        q0 = 0.25 * g[19] + 0.125 * ((g[20] + g[21]) + (g[22] + g[23]) + (g[24] + g[25]))
        q1x, q1y, q1z = (0.125 * (g[i] - g[i + 1]) for i in (20, 22, 24))
        rho, ux, uy, uz, temp = (MA[k, x] for k in range(5))
        fluid = jnp.where(SO[x] == 1, 0.0, 1.0)
        a = DE[x] * fluid
        aa = a * a
        tx = gxx * ux + gxy * uy + gxz * uz
        ty = gxy * ux + gyy * uy + gyz * uz
        tzz = gxz * ux + gyz * uy + gzz * uz
        quad = ux * tx + uy * ty + uz * tzz
        speed = ux * ux + uy * uy + uz * uz
        first_u = g1x * ux + g1y * uy + g1z * uz
        adv = q1x * ux + q1y * uy + q1z * uz
        both = 9.0 * quad - 3.0 * speed * g0
        buoy = 5.0 * a * temp / rho
        G[0, x] = 1.6 * (g0 - aa * (0.5 * both)) - buoy * adv
        G[1, x] = 1.6 * (3.0 * a * g1x + aa * (9.0 * tx - 3.0 * g0 * ux)) + buoy * q1x
        G[2, x] = 1.6 * (3.0 * a * g1y + aa * (9.0 * ty - 3.0 * g0 * uy)) + buoy * q1y
        G[3, x] = 1.6 * (3.0 * a * g1z + aa * (9.0 * tzz - 3.0 * g0 * uz)) + buoy * q1z
        hot = jnp.where(heat_lane, pltpu.roll(hT[...], lax.rem(128 - x, 128), 1), 0.0)
        G[4, x] = 1.25 * (q0 + 4.0 * a * adv) + 0.5 * hot
        term = fluid * (1.6 * rho * (3.0 * first_u + a * both) + 5.0 * temp * adv)
        reach = jnp.full((8, 128), radius[first_slab + x], jnp.int32)
        tp[x + 2] = term * jnp.where(reach == 2, 1.0 / 125.0, 1.0 / 27.0)
        return carry

    lax.fori_loop(0, nx, slab_a, 0)

    for r in (0, 1):
        tys[0, r] = tp[2 : 2 + nx, 6 + r, :]
        tys[1, r] = tp[2 : 2 + nx, r, :]
    from_lane = 126 * (1 - me_z)
    packed = jnp.zeros((8, 128), f32)
    for x in range(nx):
        moved = pltpu.roll(tp[x + 2], lax.rem(2 * x + 4 - from_lane + 128, 128), 1)
        packed = jnp.where((lane >= 2 * x + 4) & (lane < 2 * x + 6), moved, packed)
    tzs[...] = packed

    round_2 = copies(ROUND_2, refs_2, send2, recv2)
    start(ROUND_2, round_2)

    def slab_b(x, carry):
        walls = SO[x] == 1
        p, mx, my, mz, h = (G[k, x] for k in range(5))
        g = [O[i, x] for i in range(26)]
        O[0, x] = jnp.where(walls, g[0], -0.6 * g[0] + p)
        for i in range(1, 19, 2):
            cx, cy, cz = VECTORS[i]
            along = None
            for c, m in ((cx, mx), (cy, my), (cz, mz)):
                if c:
                    along = m if along is None else along + m if c > 0 else along - m
            O[i, x] = jnp.where(walls, g[i + 1], -0.6 * g[i] + (p + along))
            O[i + 1, x] = jnp.where(walls, g[i], -0.6 * g[i + 1] + (p - along))
        for i in range(19, 26):
            O[i, x] = -0.25 * g[i] + h
        return carry

    stores = []
    for n in range(4):
        lax.fori_loop(n * (nx // 4), (n + 1) * (nx // 4), slab_b, 0)
        part = pl.ds(n * (nx // 4), nx // 4)
        stores.append(pltpu.make_async_copy(O.at[:, part], out.at[:, part], out_sem.at[n]))
        stores[-1].start()

    arrive(ROUND_2, round_2)

    def along_z(v, enter, lanes, at_core):
        enter_p = jnp.where(at_core == 0, enter, 0.0)
        enter_m = jnp.where(at_core == 1, enter, 0.0)
        one = v + pltpu.roll(jnp.where(lanes == 0, enter_p, v), 127, 1)
        one = one + pltpu.roll(jnp.where(lanes == 127, enter_m, v), 1, 1)
        two = one + pltpu.roll(jnp.where(lanes < 2, enter_p, v), 126, 1)
        two = two + pltpu.roll(jnp.where(lanes >= 126, enter_m, v), 2, 1)
        return one, two

    lane_t = lax.broadcasted_iota(jnp.int32, (nx + 16, 128), 1)
    core_t = jnp.full((nx + 16, 128), me_z, jnp.int32)
    for side in (0, 1):
        for r in (0, 1):
            one, two = along_z(trow[side, r], tyz[side, r], lane_t, core_t)
            zr[0, side, r] = one
            zr[1, side, r] = two

    low = pltpu.roll(tz[1], 128 - 2 * nx, 1)
    high = pltpu.roll(tz[2], 2 * nx, 1)
    columns = jnp.where(lane < 4, low, jnp.where(lane >= 2 * nx + 4, high, tz[0]))
    tz[0] = columns

    def slab_c(n, carry):
        at = jnp.clip(first_slab + n - 2, 0, px * nx - 1)
        wide = jnp.full((8, 128), radius[at], jnp.int32) == 2
        enter = pltpu.roll(tz[0], lax.rem(126 * me_z - 2 * n + 256, 128), 1)
        one, two = along_z(tp[n], enter, lane, core)
        v = jnp.where(wide, two, one)
        here = pl.ds(6 + n, 1)
        up_1 = jnp.where(wide, zr[1, 1, 0, here, :], zr[0, 1, 0, here, :])
        up_2 = zr[1, 1, 1, here, :]
        down_1 = jnp.where(wide, zr[1, 0, 1, here, :], zr[0, 0, 1, here, :])
        down_2 = zr[1, 0, 0, here, :]
        v_up = jnp.where(sub == 0, up_1, v)
        v_down = jnp.where(sub == 7, down_1, v)
        one = v + pltpu.roll(v_up, 7, 0) + pltpu.roll(v_down, 1, 0)
        two = one + pltpu.roll(jnp.where(sub == 1, up_2, v_up), 6, 0)
        two = two + pltpu.roll(jnp.where(sub == 6, down_2, v_down), 2, 0)
        Wb[0, n] = jnp.where(wide, two, one)
        Wb[1, n] = jnp.where(wide, two, 0.0)
        return carry

    lax.fori_loop(0, nx + 4, slab_c, 0, unroll=4)
    for x in range(nx):
        SE[x] = (Wb[0, x + 1] + Wb[0, x + 2]) + (Wb[0, x + 3] + (Wb[1, x] + Wb[1, x + 4]))
    last = pltpu.make_async_copy(SE, sens, out_sem.at[4])
    last.start()
    leave(ROUND_1, round_1)
    leave(ROUND_2, round_2)
    for store in stores:
        store.wait()
    last.wait()


def body(adjoint_state, macroscopic_state, design, solid, heated, face_labels, radius):
    count, nx, ny, nz = adjoint_state.shape
    assert (count, ny, nz) == (26, 8, 128) and lax.axis_size("gz") == 2 and nx == 16
    f32 = jnp.float32
    any_space = pl.BlockSpec(memory_space=pl.ANY)
    vmem = lambda *shape: pltpu.VMEM(shape, f32)
    dma = lambda n: pltpu.SemaphoreType.DMA((n,))

    def run(*refs):
        kernel(nx, *refs)

    return pl.pallas_call(
        run,
        out_shape=(
            jax.ShapeDtypeStruct(adjoint_state.shape, f32),
            jax.ShapeDtypeStruct(design.shape, f32),
        ),
        in_specs=[any_space] * 6 + [pl.BlockSpec(memory_space=pltpu.SMEM)],
        out_specs=(any_space, any_space),
        scratch_shapes=[
            vmem(26, nx + 2, 8, 128),
            vmem(5, nx, 8, 128),
            vmem(nx, 8, 128),
            pltpu.VMEM((nx, 8, 128), jnp.int32),
            pltpu.VMEM((8, nx), jnp.int32),
            pltpu.VMEM((2, 8, 128), jnp.int32),
            vmem(26, nx, 8, 128),
            vmem(5, nx, 8, 128),
            vmem(2, 6, 8, 128),
            vmem(2, 6, 8, 128),
            vmem(2, 6, nx, 128),
            vmem(2, 6, nx + 16, 128),
            vmem(8, 128),
            vmem(8, 128),
            vmem(2, 8, 128),
            vmem(2, nx, 128),
            vmem(nx + 4, 8, 128),
            vmem(2, 2, nx, 128),
            vmem(2, 2, nx + 16, 128),
            vmem(2, 2, nx + 16, 128),
            vmem(8, 128),
            vmem(3, 8, 128),
            vmem(2, 2, 2, nx + 16, 128),
            vmem(2, nx + 4, 8, 128),
            vmem(8, 128),
            vmem(nx, 8, 128),
            dma(6), dma(5),
            dma(len(ROUND_1)), dma(len(ROUND_1)),
            dma(len(ROUND_2)), dma(len(ROUND_2)),
        ],
        compiler_params=pltpu.CompilerParams(
            collective_id=0, has_side_effects=True, vmem_limit_bytes=24 * 1024 * 1024
        ),
    )(adjoint_state, macroscopic_state, design, solid, heated.T, face_labels, radius)


def solution(mesh):
    placed = (
        P(None, ("cases", "gx"), "gy", "gz"),
        P(None, ("cases", "gx"), "gy", "gz"),
        P(("cases", "gx"), "gy", "gz"),
        P(("cases", "gx"), "gy", "gz"),
        P(("cases", "gx"), "gy"),
        P("cases", "gy", "gz"),
        P("cases"),
    )
    return jax.shard_map(
        body,
        mesh=mesh,
        in_specs=placed,
        out_specs=(P(None, ("cases", "gx"), "gy", "gz"), P(("cases", "gx"), "gy", "gz")),
        check_vma=False,
    )
```

```python
import jax
import jax.numpy as jnp
from jax import lax
from jax.experimental import pallas as pl
from jax.experimental.pallas import tpu as pltpu
from jax.sharding import PartitionSpec as P

VECTORS = [
    (0, 0, 0),
    (1, 0, 0), (-1, 0, 0), (0, 1, 0), (0, -1, 0), (0, 0, 1), (0, 0, -1),
    (1, 1, 0), (-1, -1, 0), (1, -1, 0), (-1, 1, 0),
    (1, 0, 1), (-1, 0, -1), (1, 0, -1), (-1, 0, 1),
    (0, 1, 1), (0, -1, -1), (0, 1, -1), (0, -1, 1),
]
VECTORS = VECTORS + VECTORS[:7]
OPP = [0, 2, 1, 4, 3, 6, 5, 8, 7, 10, 9, 12, 11, 14, 13, 16, 15, 18, 17, 19, 21, 20, 23, 22, 25, 24]
X_FROM = ([2, 8, 10, 12, 14, 21], [1, 7, 9, 11, 13, 20])
Y_FROM = ([4, 8, 9, 16, 18, 23], [3, 7, 10, 15, 17, 22])
Z_PAIRS = [(5, 6, 0), (15, 17, 16), (18, 16, 32), (24, 25, 48), (11, 13, 64), (14, 12, 96)]
Z_BASE = {i: base for a, b, base in Z_PAIRS for i in (a, b)}
MESH = pl.DeviceIdType.MESH
W0, W1, W2 = 1.0 / 3.0, 1.0 / 18.0, 1.0 / 36.0

ROUND_1 = (
    [(dx, 0, 0) for dx in (1, -1)]
    + [(0, dy, 0) for dy in (1, -1)]
    + [(0, 0, 1)]
    + [(dx, dy, 0) for dx in (1, -1) for dy in (1, -1)]
    + [(dx, 0, 1) for dx in (1, -1)]
    + [(0, dy, 1) for dy in (1, -1)]
)
ROUND_2 = ROUND_1 + [(dx, dy, 1) for dx in (1, -1) for dy in (1, -1)]


def kernel(
    nx, state, macro, design, solid, heated, faces, radius, out, sens,
    S, MA, DE, SO, HE, FA, O, xs, xr, ys, yh, zs, zh, xzr, yzr,
    tp, tys, trow, tyz, tzs, tz, zr, Wb, hT, SE,
    in_sem, out_sem, send1, recv1, send2, recv2,
):
    f32 = jnp.float32
    px, py = lax.axis_size("gx"), lax.axis_size("gy")
    me_c, me_x = lax.axis_index("cases"), lax.axis_index("gx")
    me_y, me_z = lax.axis_index("gy"), lax.axis_index("gz")

    def has(d):
        flag = None
        for delta, me, count in ((d[0], me_x, px), (d[1], me_y, py)):
            if delta == 0:
                continue
            here = me < count - 1 if delta > 0 else me > 0
            flag = here if flag is None else jnp.logical_and(flag, here)
        return flag

    def when(flag, body):
        if flag is None:
            body()
        else:
            pl.when(flag)(body)

    def target(d):
        return (me_c, me_x + d[0], me_y + d[1], 1 - me_z if d[2] else me_z)

    loads = [
        pltpu.make_async_copy(state, S.at[:, 1 : 1 + nx], in_sem.at[0]),
        pltpu.make_async_copy(macro, MA, in_sem.at[1]),
        pltpu.make_async_copy(design, DE, in_sem.at[2]),
        pltpu.make_async_copy(solid, SO, in_sem.at[3]),
        pltpu.make_async_copy(heated, HE, in_sem.at[4]),
        pltpu.make_async_copy(faces, FA, in_sem.at[5]),
    ]
    for load in loads:
        load.start()

    trow[...] = jnp.zeros_like(trow)
    tyz[...] = jnp.zeros_like(tyz)
    tz[...] = jnp.zeros_like(tz)
    tp[0:2] = jnp.zeros((2, 8, 128), f32)
    tp[nx + 2 : nx + 4] = jnp.zeros((2, 8, 128), f32)

    barrier = pltpu.get_barrier_semaphore()
    for d in ROUND_2:
        def greet(d=d):
            pl.semaphore_signal(barrier, inc=1, device_id=target(d), device_id_type=MESH)
        when(has(d), greet)

    lane = lax.broadcasted_iota(jnp.int32, (8, 128), 1)
    sub = lax.broadcasted_iota(jnp.int32, (8, 128), 0)
    edge = 127 * me_z
    mine = 127 - edge

    for load in loads:
        load.wait()

    for side, (x_at, y_at) in enumerate(((nx, 7), (1, 0))):
        for j in range(6):
            xs[side, j] = S[X_FROM[side][j], x_at]
            ys[side, j] = S[Y_FROM[side][j], 1 : 1 + nx, y_at, :]

    def pack(x, acc):
        for first, second, base in Z_PAIRS:
            v = S[jnp.where(me_z == 1, first, second), x + 1]
            moved = pltpu.roll(v, lax.rem(base + x - mine + 256, 128), 1)
            acc = jnp.where(lane == base + x, moved, acc)
        return acc

    zs[...] = lax.fori_loop(0, nx, pack, jnp.zeros((8, 128), f32), unroll=True)

    beside_x = jnp.where(me_x > 0, 1, 0) + jnp.where(me_x < px - 1, 1, 0)
    beside_y = jnp.where(me_y > 0, 1, 0) + jnp.where(me_y < py - 1, 1, 0)
    pl.semaphore_wait(barrier, 2 * (beside_x + 1) * (beside_y + 1) - 1)

    def refs_1(d):
        dx, dy, dz = d
        side_x, side_y = (0 if dx > 0 else 1), (0 if dy > 0 else 1)
        if dx and dy:
            j = next(k for k, i in enumerate(Y_FROM[side_y]) if VECTORS[i][0] == -dx)
            if dx > 0:
                return ys.at[side_y, j, nx - 8 : nx], yh.at[side_y, j, 0:8]
            return ys.at[side_y, j, 0:8], yh.at[side_y, j, nx + 8 : nx + 16]
        if dx and dz:
            pair = (14, 12) if dx > 0 else (11, 13)
            return S.at[jnp.where(me_z == 1, pair[0], pair[1]), nx if dx > 0 else 1], xzr.at[side_x]
        if dy and dz:
            j = jnp.where(me_z == 1, 4, 3) if dy > 0 else jnp.where(me_z == 1, 3, 4)
            return ys.at[side_y, j], yzr.at[side_y]
        if dx:
            return xs.at[side_x], xr.at[side_x]
        if dy:
            return ys.at[side_y], yh.at[side_y, :, 8 : 8 + nx]
        return zs, zh

    def refs_2(d):
        dx, dy, dz = d
        side_y = 0 if dy > 0 else 1
        if dy:
            into = tyz if dz else trow
            if dx > 0:
                return tys.at[side_y, :, nx - 8 : nx], into.at[side_y, :, 0:8]
            if dx < 0:
                return tys.at[side_y, :, 0:8], into.at[side_y, :, nx + 8 : nx + 16]
            return tys.at[side_y], into.at[side_y, :, 8 : 8 + nx]
        if dz:
            return tzs, tz.at[0 if dx == 0 else 1 if dx > 0 else 2]
        if dx > 0:
            return tp.at[nx : nx + 2], tp.at[0:2]
        return tp.at[2:4], tp.at[nx + 2 : nx + 4]

    def copies(messages, refs, sends, recvs):
        made = []
        for n, d in enumerate(messages):
            src, dst = refs(d)
            made.append(
                pltpu.make_async_remote_copy(
                    src_ref=src, dst_ref=dst, send_sem=sends.at[n], recv_sem=recvs.at[n],
                    device_id=target(d), device_id_type=MESH,
                )
            )
        return made

    def start(messages, made):
        for d, copy in zip(messages, made):
            when(has(d), copy.start)

    def arrive(messages, made):
        for d, copy in zip(messages, made):
            when(has((-d[0], -d[1], d[2])), copy.wait_recv)

    def leave(messages, made):
        for d, copy in zip(messages, made):
            when(has(d), copy.wait_send)

    round_1 = copies(ROUND_1, refs_1, send1, recv1)
    start(ROUND_1, round_1)

    hT[...] = jnp.zeros_like(hT)
    hT[:, 0:nx] = jnp.where(HE[...] == 1, 1.0, 0.0)

    core = jnp.full((8, 128), me_z, jnp.int32)
    col_p = (lane == 0) & (core == 0)
    col_m = (lane == 127) & (core == 1)
    out_z = {1: (lane == 127) & (core == 1), -1: (lane == 0) & (core == 0)}
    at_y = jnp.full((8, 128), me_y, jnp.int32)
    out_y = {1: (sub == 7) & (at_y == py - 1), -1: (sub == 0) & (at_y == 0)}
    face = {1: FA[1] == 1, -1: FA[0] == 1}
    heat_lane = (lane == 0) & (core == 0)

    arrive(ROUND_1, round_1)

    for side, at in ((0, 0), (1, nx + 1)):
        for j in range(6):
            S[X_FROM[side][j], at] = xr[side, j]
    lane_r = lax.broadcasted_iota(jnp.int32, (nx, 128), 1)
    core_r = jnp.full((nx, 128), me_z, jnp.int32)
    for side in (0, 1):
        for j in (3, 4):
            up = VECTORS[Y_FROM[side][j]][2] > 0
            mask = (lane_r == (0 if up else 127)) & (core_r == (0 if up else 1))
            yh[side, j, 8 : 8 + nx] = jnp.where(mask, yzr[side], yh[side, j, 8 : 8 + nx])
    cols = zh[...]
    cols = jnp.where(lane == 80, pltpu.roll(xzr[1], lax.rem(80 - edge + 128, 128), 1), cols)
    cols = jnp.where(lane == 95, pltpu.roll(xzr[0], lax.rem(95 - edge + 128, 128), 1), cols)
    zh[...] = cols

    first_slab = me_x * nx

    def slab_a(x, carry):
        cols = zh[...]
        at_x = jnp.full((8, 128), first_slab + x, jnp.int32)
        out_x = {1: at_x == px * nx - 1, -1: at_x == 0}
        column = {}
        for first, second, base in Z_PAIRS:
            k = base + x + VECTORS[first][0]
            column[base] = pltpu.roll(cols, lax.rem(edge - k + 256, 128), 1)
        g = []
        for i in range(26):
            cx, cy, cz = VECTORS[i]
            v = S[i, x + 1 + cx]
            if cz:
                v = jnp.where(col_p if cz > 0 else col_m, column[Z_BASE[i]], v)
            if cy:
                side = 0 if cy < 0 else 1
                row = yh[side, Y_FROM[side].index(i), pl.ds(8 + x + cx, 1), :]
                v = jnp.where(sub == (0 if cy > 0 else 7), row, v)
                v = pltpu.roll(v, 7 if cy > 0 else 1, 0)
            if cz:
                v = pltpu.roll(v, 127 if cz > 0 else 1, 1)
            if (cx, cy, cz) != (0, 0, 0):
                bounce = S[OPP[i], x + 1]
                leaves = None
                if cy:
                    leaves = out_y[cy]
                if cz:
                    leaves = out_z[cz] if leaves is None else leaves | out_z[cz]
                if cx:
                    opened = out_x[cx] & face[cx]
                    if leaves is not None:
                        opened = opened & jnp.logical_not(leaves)
                    bounce = jnp.where(opened, 0.0, bounce)
                    leaves = out_x[cx] if leaves is None else leaves | out_x[cx]
                v = jnp.where(leaves, bounce, v)
            O[i, x] = v
            g.append(v)
        s = {i: g[i] + g[i + 1] for i in range(1, 19, 2)}
        d = {i: g[i] - g[i + 1] for i in range(1, 19, 2)}
        xy, xz, yz = s[7] + s[9], s[11] + s[13], s[15] + s[17]
        g0 = W0 * g[0] + W1 * (s[1] + s[3] + s[5]) + W2 * (xy + xz + yz)
        g1x = W1 * d[1] + W2 * ((d[7] + d[9]) + (d[11] + d[13]))
        g1y = W1 * d[3] + W2 * ((d[7] - d[9]) + (d[15] + d[17]))
        g1z = W1 * d[5] + W2 * ((d[11] - d[13]) + (d[15] - d[17]))
        gxx = W1 * s[1] + W2 * (xy + xz)
        gyy = W1 * s[3] + W2 * (xy + yz)
        gzz = W1 * s[5] + W2 * (xz + yz)
        gxy, gxz, gyz = W2 * (s[7] - s[9]), W2 * (s[11] - s[13]), W2 * (s[15] - s[17])
        q0 = 0.25 * g[19] + 0.125 * ((g[20] + g[21]) + (g[22] + g[23]) + (g[24] + g[25]))
        q1x, q1y, q1z = (0.125 * (g[i] - g[i + 1]) for i in (20, 22, 24))
        rho, ux, uy, uz, temp = (MA[k, x] for k in range(5))
        fluid = jnp.where(SO[x] == 1, 0.0, 1.0)
        a = DE[x] * fluid
        aa = a * a
        tx = gxx * ux + gxy * uy + gxz * uz
        ty = gxy * ux + gyy * uy + gyz * uz
        tzz = gxz * ux + gyz * uy + gzz * uz
        quad = ux * tx + uy * ty + uz * tzz
        speed = ux * ux + uy * uy + uz * uz
        first_u = g1x * ux + g1y * uy + g1z * uz
        adv = q1x * ux + q1y * uy + q1z * uz
        both = 9.0 * quad - 3.0 * speed * g0
        buoy = 5.0 * a * temp / rho
        O[26, x] = 1.6 * (g0 - aa * (0.5 * both)) - buoy * adv
        O[27, x] = 1.6 * (3.0 * a * g1x + aa * (9.0 * tx - 3.0 * g0 * ux)) + buoy * q1x
        O[28, x] = 1.6 * (3.0 * a * g1y + aa * (9.0 * ty - 3.0 * g0 * uy)) + buoy * q1y
        O[29, x] = 1.6 * (3.0 * a * g1z + aa * (9.0 * tzz - 3.0 * g0 * uz)) + buoy * q1z
        hot = jnp.where(heat_lane, pltpu.roll(hT[...], lax.rem(128 - x, 128), 1), 0.0)
        O[30, x] = 1.25 * (q0 + 4.0 * a * adv) + 0.5 * hot
        term = fluid * (1.6 * rho * (3.0 * first_u + a * both) + 5.0 * temp * adv)
        reach = jnp.full((8, 128), radius[first_slab + x], jnp.int32)
        tp[x + 2] = term * jnp.where(reach == 2, 1.0 / 125.0, 1.0 / 27.0)
        return carry

    stores = []
    for n in range(4):
        lax.fori_loop(n * (nx // 4), (n + 1) * (nx // 4), slab_a, 0, unroll=4)
        part = pl.ds(n * (nx // 4), nx // 4)
        stores.append(pltpu.make_async_copy(O.at[:, part], out.at[:, part], out_sem.at[n]))
        stores[-1].start()

    for r in (0, 1):
        tys[0, r] = tp[2 : 2 + nx, 6 + r, :]
        tys[1, r] = tp[2 : 2 + nx, r, :]
    from_lane = 126 * (1 - me_z)
    packed = jnp.zeros((8, 128), f32)
    for x in range(nx):
        moved = pltpu.roll(tp[x + 2], lax.rem(2 * x + 4 - from_lane + 128, 128), 1)
        packed = jnp.where((lane >= 2 * x + 4) & (lane < 2 * x + 6), moved, packed)
    tzs[...] = packed

    round_2 = copies(ROUND_2, refs_2, send2, recv2)
    start(ROUND_2, round_2)

    arrive(ROUND_2, round_2)

    def along_z(v, enter, lanes, at_core):
        enter_p = jnp.where(at_core == 0, enter, 0.0)
        enter_m = jnp.where(at_core == 1, enter, 0.0)
        one = v + pltpu.roll(jnp.where(lanes == 0, enter_p, v), 127, 1)
        one = one + pltpu.roll(jnp.where(lanes == 127, enter_m, v), 1, 1)
        two = one + pltpu.roll(jnp.where(lanes < 2, enter_p, v), 126, 1)
        two = two + pltpu.roll(jnp.where(lanes >= 126, enter_m, v), 2, 1)
        return one, two

    lane_t = lax.broadcasted_iota(jnp.int32, (nx + 16, 128), 1)
    core_t = jnp.full((nx + 16, 128), me_z, jnp.int32)
    for side in (0, 1):
        for r in (0, 1):
            one, two = along_z(trow[side, r], tyz[side, r], lane_t, core_t)
            zr[0, side, r] = one
            zr[1, side, r] = two

    low = pltpu.roll(tz[1], 128 - 2 * nx, 1)
    high = pltpu.roll(tz[2], 2 * nx, 1)
    columns = jnp.where(lane < 4, low, jnp.where(lane >= 2 * nx + 4, high, tz[0]))
    tz[0] = columns

    def slab_c(n, carry):
        at = jnp.clip(first_slab + n - 2, 0, px * nx - 1)
        wide = jnp.full((8, 128), radius[at], jnp.int32) == 2
        enter = pltpu.roll(tz[0], lax.rem(126 * me_z - 2 * n + 256, 128), 1)
        one, two = along_z(tp[n], enter, lane, core)
        v = jnp.where(wide, two, one)
        here = pl.ds(6 + n, 1)
        up_1 = jnp.where(wide, zr[1, 1, 0, here, :], zr[0, 1, 0, here, :])
        up_2 = zr[1, 1, 1, here, :]
        down_1 = jnp.where(wide, zr[1, 0, 1, here, :], zr[0, 0, 1, here, :])
        down_2 = zr[1, 0, 0, here, :]
        v_up = jnp.where(sub == 0, up_1, v)
        v_down = jnp.where(sub == 7, down_1, v)
        one = v + pltpu.roll(v_up, 7, 0) + pltpu.roll(v_down, 1, 0)
        two = one + pltpu.roll(jnp.where(sub == 1, up_2, v_up), 6, 0)
        two = two + pltpu.roll(jnp.where(sub == 6, down_2, v_down), 2, 0)
        Wb[0, n] = jnp.where(wide, two, one)
        Wb[1, n] = jnp.where(wide, two, 0.0)
        return carry

    lax.fori_loop(0, nx + 4, slab_c, 0, unroll=4)
    for x in range(nx):
        SE[x] = (Wb[0, x + 1] + Wb[0, x + 2]) + (Wb[0, x + 3] + (Wb[1, x] + Wb[1, x + 4]))
    last = pltpu.make_async_copy(SE, sens, out_sem.at[4])
    last.start()
    leave(ROUND_1, round_1)
    leave(ROUND_2, round_2)
    for store in stores:
        store.wait()
    last.wait()


def finish(pulled, solid, sens_in, out, sens):
    for x in range(solid.shape[0]):
        walls = solid[x] == 1
        p, mx, my, mz, h = (pulled[26 + k, x] for k in range(5))
        g = [pulled[i, x] for i in range(26)]
        out[0, x] = jnp.where(walls, g[0], -0.6 * g[0] + p)
        for i in range(1, 19, 2):
            cx, cy, cz = VECTORS[i]
            along = None
            for c, m in ((cx, mx), (cy, my), (cz, mz)):
                if c:
                    along = m if along is None else along + m if c > 0 else along - m
            out[i, x] = jnp.where(walls, g[i + 1], -0.6 * g[i] + (p + along))
            out[i + 1, x] = jnp.where(walls, g[i], -0.6 * g[i + 1] + (p - along))
        for i in range(19, 26):
            out[i, x] = -0.25 * g[i] + h
    sens[...] = sens_in[...]


def body(adjoint_state, macroscopic_state, design, solid, heated, face_labels, radius):
    count, nx, ny, nz = adjoint_state.shape
    assert (count, ny, nz) == (26, 8, 128) and lax.axis_size("gz") == 2 and nx == 16
    f32 = jnp.float32
    any_space = pl.BlockSpec(memory_space=pl.ANY)
    vmem = lambda *shape: pltpu.VMEM(shape, f32)
    dma = lambda n: pltpu.SemaphoreType.DMA((n,))

    def run(*refs):
        kernel(nx, *refs)

    pulled, sens = pl.pallas_call(
        run,
        out_shape=(
            jax.ShapeDtypeStruct((31,) + design.shape, f32),
            jax.ShapeDtypeStruct(design.shape, f32),
        ),
        in_specs=[any_space] * 6 + [pl.BlockSpec(memory_space=pltpu.SMEM)],
        out_specs=(any_space, any_space),
        scratch_shapes=[
            vmem(26, nx + 2, 8, 128),
            vmem(5, nx, 8, 128),
            vmem(nx, 8, 128),
            pltpu.VMEM((nx, 8, 128), jnp.int32),
            pltpu.VMEM((8, nx), jnp.int32),
            pltpu.VMEM((2, 8, 128), jnp.int32),
            vmem(31, nx, 8, 128),
            vmem(2, 6, 8, 128),
            vmem(2, 6, 8, 128),
            vmem(2, 6, nx, 128),
            vmem(2, 6, nx + 16, 128),
            vmem(8, 128),
            vmem(8, 128),
            vmem(2, 8, 128),
            vmem(2, nx, 128),
            vmem(nx + 4, 8, 128),
            vmem(2, 2, nx, 128),
            vmem(2, 2, nx + 16, 128),
            vmem(2, 2, nx + 16, 128),
            vmem(8, 128),
            vmem(3, 8, 128),
            vmem(2, 2, 2, nx + 16, 128),
            vmem(2, nx + 4, 8, 128),
            vmem(8, 128),
            vmem(nx, 8, 128),
            dma(6), dma(5),
            dma(len(ROUND_1)), dma(len(ROUND_1)),
            dma(len(ROUND_2)), dma(len(ROUND_2)),
        ],
        compiler_params=pltpu.CompilerParams(
            collective_id=0, has_side_effects=True, vmem_limit_bytes=56 * 1024 * 1024
        ),
    )(adjoint_state, macroscopic_state, design, solid, heated.T, face_labels, radius)
    step = 8
    cells = pl.BlockSpec((step, 8, 128), lambda n: (n, 0, 0))
    block = lambda count: pl.BlockSpec((count, step, 8, 128), lambda n: (0, n, 0, 0))
    return pl.pallas_call(
        finish,
        grid=(nx // step,),
        out_shape=(
            jax.ShapeDtypeStruct(adjoint_state.shape, f32),
            jax.ShapeDtypeStruct(design.shape, f32),
        ),
        in_specs=[block(31), cells, cells],
        out_specs=(block(26), cells),
        compiler_params=pltpu.CompilerParams(vmem_limit_bytes=56 * 1024 * 1024),
    )(pulled, solid, sens)


def solution(mesh):
    placed = (
        P(None, ("cases", "gx"), "gy", "gz"),
        P(None, ("cases", "gx"), "gy", "gz"),
        P(("cases", "gx"), "gy", "gz"),
        P(("cases", "gx"), "gy", "gz"),
        P(("cases", "gx"), "gy"),
        P("cases", "gy", "gz"),
        P("cases"),
    )
    return jax.shard_map(
        body,
        mesh=mesh,
        in_specs=placed,
        out_specs=(P(None, ("cases", "gx"), "gy", "gz"), P(("cases", "gx"), "gy", "gz")),
        check_vma=False,
    )
```

```python
import jax
import jax.numpy as jnp
from jax import lax
from jax.experimental import pallas as pl
from jax.experimental.pallas import tpu as pltpu
from jax.sharding import PartitionSpec as P

VECTORS = [
    (0, 0, 0),
    (1, 0, 0), (-1, 0, 0), (0, 1, 0), (0, -1, 0), (0, 0, 1), (0, 0, -1),
    (1, 1, 0), (-1, -1, 0), (1, -1, 0), (-1, 1, 0),
    (1, 0, 1), (-1, 0, -1), (1, 0, -1), (-1, 0, 1),
    (0, 1, 1), (0, -1, -1), (0, 1, -1), (0, -1, 1),
]
VECTORS = VECTORS + VECTORS[:7]
OPP = [0, 2, 1, 4, 3, 6, 5, 8, 7, 10, 9, 12, 11, 14, 13, 16, 15, 18, 17, 19, 21, 20, 23, 22, 25, 24]
X_FROM = ([2, 8, 10, 12, 14, 21], [1, 7, 9, 11, 13, 20])
Y_FROM = ([4, 8, 9, 16, 18, 23], [3, 7, 10, 15, 17, 22])
Z_PAIRS = [(5, 6, 0), (15, 17, 16), (18, 16, 32), (24, 25, 48), (11, 13, 64), (14, 12, 96)]
Z_BASE = {i: base for a, b, base in Z_PAIRS for i in (a, b)}
MESH = pl.DeviceIdType.MESH
W0, W1, W2 = 1.0 / 3.0, 1.0 / 18.0, 1.0 / 36.0

ROUND_1 = (
    [(dx, 0, 0) for dx in (1, -1)]
    + [(0, dy, 0) for dy in (1, -1)]
    + [(0, 0, 1)]
    + [(dx, dy, 0) for dx in (1, -1) for dy in (1, -1)]
    + [(dx, 0, 1) for dx in (1, -1)]
    + [(0, dy, 1) for dy in (1, -1)]
)
ROUND_1 = ROUND_1[5:] + ROUND_1[2:4] + ROUND_1[:2] + ROUND_1[4:5]
ROUND_2 = [(dx, dy, 1) for dx in (1, -1) for dy in (1, -1)] + ROUND_1


def kernel(
    nx, state, macro, design, solid, heated, faces, radius, out, sens,
    S, MA, DE, SO, HE, FA, O, xs, xr, ys, yh, zs, zh, xzr, yzr,
    tp, tys, trow, tyz, tzs, tz, zr, Wb, hT, SE,
    in_sem, out_sem, send1, recv1, send2, recv2,
):
    f32 = jnp.float32
    px, py = lax.axis_size("gx"), lax.axis_size("gy")
    me_c, me_x = lax.axis_index("cases"), lax.axis_index("gx")
    me_y, me_z = lax.axis_index("gy"), lax.axis_index("gz")

    def has(d):
        flag = None
        for delta, me, count in ((d[0], me_x, px), (d[1], me_y, py)):
            if delta == 0:
                continue
            here = me < count - 1 if delta > 0 else me > 0
            flag = here if flag is None else jnp.logical_and(flag, here)
        return flag

    def when(flag, body):
        if flag is None:
            body()
        else:
            pl.when(flag)(body)

    def target(d):
        return (me_c, me_x + d[0], me_y + d[1], 1 - me_z if d[2] else me_z)

    loads = [
        pltpu.make_async_copy(state, S.at[:, 1 : 1 + nx], in_sem.at[0]),
        pltpu.make_async_copy(macro, MA, in_sem.at[1]),
        pltpu.make_async_copy(design, DE, in_sem.at[2]),
        pltpu.make_async_copy(solid, SO, in_sem.at[3]),
        pltpu.make_async_copy(heated, HE, in_sem.at[4]),
        pltpu.make_async_copy(faces, FA, in_sem.at[5]),
    ]
    for load in loads:
        load.start()

    trow[...] = jnp.zeros_like(trow)
    tyz[...] = jnp.zeros_like(tyz)
    tz[...] = jnp.zeros_like(tz)
    tp[0:2] = jnp.zeros((2, 8, 128), f32)
    tp[nx + 2 : nx + 4] = jnp.zeros((2, 8, 128), f32)

    barrier = pltpu.get_barrier_semaphore()
    for d in ROUND_2:
        def greet(d=d):
            pl.semaphore_signal(barrier, inc=1, device_id=target(d), device_id_type=MESH)
        when(has(d), greet)

    lane = lax.broadcasted_iota(jnp.int32, (8, 128), 1)
    sub = lax.broadcasted_iota(jnp.int32, (8, 128), 0)
    edge = 127 * me_z
    mine = 127 - edge

    for load in loads:
        load.wait()

    for side, (x_at, y_at) in enumerate(((nx, 7), (1, 0))):
        for j in range(6):
            xs[side, j] = S[X_FROM[side][j], x_at]
            ys[side, j] = S[Y_FROM[side][j], 1 : 1 + nx, y_at, :]

    def pack(x, acc):
        for first, second, base in Z_PAIRS:
            v = S[jnp.where(me_z == 1, first, second), x + 1]
            moved = pltpu.roll(v, lax.rem(base + x - mine + 256, 128), 1)
            acc = jnp.where(lane == base + x, moved, acc)
        return acc

    zs[...] = lax.fori_loop(0, nx, pack, jnp.zeros((8, 128), f32), unroll=True)

    beside_x = jnp.where(me_x > 0, 1, 0) + jnp.where(me_x < px - 1, 1, 0)
    beside_y = jnp.where(me_y > 0, 1, 0) + jnp.where(me_y < py - 1, 1, 0)
    pl.semaphore_wait(barrier, 2 * (beside_x + 1) * (beside_y + 1) - 1)

    def refs_1(d):
        dx, dy, dz = d
        side_x, side_y = (0 if dx > 0 else 1), (0 if dy > 0 else 1)
        if dx and dy:
            j = next(k for k, i in enumerate(Y_FROM[side_y]) if VECTORS[i][0] == -dx)
            if dx > 0:
                return ys.at[side_y, j, nx - 8 : nx], yh.at[side_y, j, 0:8]
            return ys.at[side_y, j, 0:8], yh.at[side_y, j, nx + 8 : nx + 16]
        if dx and dz:
            pair = (14, 12) if dx > 0 else (11, 13)
            return S.at[jnp.where(me_z == 1, pair[0], pair[1]), nx if dx > 0 else 1], xzr.at[side_x]
        if dy and dz:
            j = jnp.where(me_z == 1, 4, 3) if dy > 0 else jnp.where(me_z == 1, 3, 4)
            return ys.at[side_y, j], yzr.at[side_y]
        if dx:
            return xs.at[side_x], xr.at[side_x]
        if dy:
            return ys.at[side_y], yh.at[side_y, :, 8 : 8 + nx]
        return zs, zh

    def refs_2(d):
        dx, dy, dz = d
        side_y = 0 if dy > 0 else 1
        if dy:
            into = tyz if dz else trow
            if dx > 0:
                return tys.at[side_y, :, nx - 8 : nx], into.at[side_y, :, 0:8]
            if dx < 0:
                return tys.at[side_y, :, 0:8], into.at[side_y, :, nx + 8 : nx + 16]
            return tys.at[side_y], into.at[side_y, :, 8 : 8 + nx]
        if dz:
            return tzs, tz.at[0 if dx == 0 else 1 if dx > 0 else 2]
        if dx > 0:
            return tp.at[nx : nx + 2], tp.at[0:2]
        return tp.at[2:4], tp.at[nx + 2 : nx + 4]

    def copies(messages, refs, sends, recvs):
        made = []
        for n, d in enumerate(messages):
            src, dst = refs(d)
            made.append(
                pltpu.make_async_remote_copy(
                    src_ref=src, dst_ref=dst, send_sem=sends.at[n], recv_sem=recvs.at[n],
                    device_id=target(d), device_id_type=MESH,
                )
            )
        return made

    def start(messages, made):
        for d, copy in zip(messages, made):
            when(has(d), copy.start)

    def arrive(messages, made):
        for d, copy in zip(messages, made):
            when(has((-d[0], -d[1], d[2])), copy.wait_recv)

    def leave(messages, made):
        for d, copy in zip(messages, made):
            when(has(d), copy.wait_send)

    round_1 = copies(ROUND_1, refs_1, send1, recv1)
    start(ROUND_1, round_1)

    hT[...] = jnp.zeros_like(hT)
    hT[:, 0:nx] = jnp.where(HE[...] == 1, 1.0, 0.0)

    core = jnp.full((8, 128), me_z, jnp.int32)
    col_p = (lane == 0) & (core == 0)
    col_m = (lane == 127) & (core == 1)
    out_z = {1: (lane == 127) & (core == 1), -1: (lane == 0) & (core == 0)}
    at_y = jnp.full((8, 128), me_y, jnp.int32)
    out_y = {1: (sub == 7) & (at_y == py - 1), -1: (sub == 0) & (at_y == 0)}
    face = {1: FA[1] == 1, -1: FA[0] == 1}
    heat_lane = (lane == 0) & (core == 0)

    arrive(ROUND_1, round_1)

    for side, at in ((0, 0), (1, nx + 1)):
        for j in range(6):
            S[X_FROM[side][j], at] = xr[side, j]
    lane_r = lax.broadcasted_iota(jnp.int32, (nx, 128), 1)
    core_r = jnp.full((nx, 128), me_z, jnp.int32)
    for side in (0, 1):
        for j in (3, 4):
            up = VECTORS[Y_FROM[side][j]][2] > 0
            mask = (lane_r == (0 if up else 127)) & (core_r == (0 if up else 1))
            yh[side, j, 8 : 8 + nx] = jnp.where(mask, yzr[side], yh[side, j, 8 : 8 + nx])
    cols = zh[...]
    cols = jnp.where(lane == 80, pltpu.roll(xzr[1], lax.rem(80 - edge + 128, 128), 1), cols)
    cols = jnp.where(lane == 95, pltpu.roll(xzr[0], lax.rem(95 - edge + 128, 128), 1), cols)
    zh[...] = cols

    first_slab = me_x * nx

    def slab_a(x, carry):
        cols = zh[...]
        at_x = jnp.full((8, 128), first_slab + x, jnp.int32)
        out_x = {1: at_x == px * nx - 1, -1: at_x == 0}
        column = {}
        for first, second, base in Z_PAIRS:
            k = base + x + VECTORS[first][0]
            column[base] = pltpu.roll(cols, lax.rem(edge - k + 256, 128), 1)
        g = []
        for i in range(26):
            cx, cy, cz = VECTORS[i]
            v = S[i, x + 1 + cx]
            if cz:
                v = jnp.where(col_p if cz > 0 else col_m, column[Z_BASE[i]], v)
            if cy:
                side = 0 if cy < 0 else 1
                row = yh[side, Y_FROM[side].index(i), pl.ds(8 + x + cx, 1), :]
                v = jnp.where(sub == (0 if cy > 0 else 7), row, v)
                v = pltpu.roll(v, 7 if cy > 0 else 1, 0)
            if cz:
                v = pltpu.roll(v, 127 if cz > 0 else 1, 1)
            if (cx, cy, cz) != (0, 0, 0):
                bounce = S[OPP[i], x + 1]
                leaves = None
                if cy:
                    leaves = out_y[cy]
                if cz:
                    leaves = out_z[cz] if leaves is None else leaves | out_z[cz]
                if cx:
                    opened = out_x[cx] & face[cx]
                    if leaves is not None:
                        opened = opened & jnp.logical_not(leaves)
                    bounce = jnp.where(opened, 0.0, bounce)
                    leaves = out_x[cx] if leaves is None else leaves | out_x[cx]
                v = jnp.where(leaves, bounce, v)
            O[i, x] = v
            g.append(v)
        s = {i: g[i] + g[i + 1] for i in range(1, 19, 2)}
        d = {i: g[i] - g[i + 1] for i in range(1, 19, 2)}
        xy, xz, yz = s[7] + s[9], s[11] + s[13], s[15] + s[17]
        g0 = W0 * g[0] + W1 * (s[1] + s[3] + s[5]) + W2 * (xy + xz + yz)
        g1x = W1 * d[1] + W2 * ((d[7] + d[9]) + (d[11] + d[13]))
        g1y = W1 * d[3] + W2 * ((d[7] - d[9]) + (d[15] + d[17]))
        g1z = W1 * d[5] + W2 * ((d[11] - d[13]) + (d[15] - d[17]))
        gxx = W1 * s[1] + W2 * (xy + xz)
        gyy = W1 * s[3] + W2 * (xy + yz)
        gzz = W1 * s[5] + W2 * (xz + yz)
        gxy, gxz, gyz = W2 * (s[7] - s[9]), W2 * (s[11] - s[13]), W2 * (s[15] - s[17])
        q0 = 0.25 * g[19] + 0.125 * ((g[20] + g[21]) + (g[22] + g[23]) + (g[24] + g[25]))
        q1x, q1y, q1z = (0.125 * (g[i] - g[i + 1]) for i in (20, 22, 24))
        rho, ux, uy, uz, temp = (MA[k, x] for k in range(5))
        fluid = jnp.where(SO[x] == 1, 0.0, 1.0)
        a = DE[x] * fluid
        aa = a * a
        tx = gxx * ux + gxy * uy + gxz * uz
        ty = gxy * ux + gyy * uy + gyz * uz
        tzz = gxz * ux + gyz * uy + gzz * uz
        quad = ux * tx + uy * ty + uz * tzz
        speed = ux * ux + uy * uy + uz * uz
        first_u = g1x * ux + g1y * uy + g1z * uz
        adv = q1x * ux + q1y * uy + q1z * uz
        both = 9.0 * quad - 3.0 * speed * g0
        buoy = 5.0 * a * temp / rho
        O[26, x] = 1.6 * (g0 - aa * (0.5 * both)) - buoy * adv
        O[27, x] = 1.6 * (3.0 * a * g1x + aa * (9.0 * tx - 3.0 * g0 * ux)) + buoy * q1x
        O[28, x] = 1.6 * (3.0 * a * g1y + aa * (9.0 * ty - 3.0 * g0 * uy)) + buoy * q1y
        O[29, x] = 1.6 * (3.0 * a * g1z + aa * (9.0 * tzz - 3.0 * g0 * uz)) + buoy * q1z
        hot = jnp.where(heat_lane, pltpu.roll(hT[...], lax.rem(128 - x, 128), 1), 0.0)
        O[30, x] = 1.25 * (q0 + 4.0 * a * adv) + 0.5 * hot
        term = fluid * (1.6 * rho * (3.0 * first_u + a * both) + 5.0 * temp * adv)
        reach = jnp.full((8, 128), radius[first_slab + x], jnp.int32)
        tp[x + 2] = term * jnp.where(reach == 2, 1.0 / 125.0, 1.0 / 27.0)
        return carry

    stores = []
    for n in range(4):
        lax.fori_loop(n * (nx // 4), (n + 1) * (nx // 4), slab_a, 0, unroll=4)
        part = pl.ds(n * (nx // 4), nx // 4)
        stores.append(pltpu.make_async_copy(O.at[:, part], out.at[:, part], out_sem.at[n]))
        stores[-1].start()

    for r in (0, 1):
        tys[0, r] = tp[2 : 2 + nx, 6 + r, :]
        tys[1, r] = tp[2 : 2 + nx, r, :]
    from_lane = 126 * (1 - me_z)
    packed = jnp.zeros((8, 128), f32)
    for x in range(nx):
        moved = pltpu.roll(tp[x + 2], lax.rem(2 * x + 4 - from_lane + 128, 128), 1)
        packed = jnp.where((lane >= 2 * x + 4) & (lane < 2 * x + 6), moved, packed)
    tzs[...] = packed

    round_2 = copies(ROUND_2, refs_2, send2, recv2)
    start(ROUND_2, round_2)

    arrive(ROUND_2, round_2)

    def along_z(v, enter, lanes, at_core):
        enter_p = jnp.where(at_core == 0, enter, 0.0)
        enter_m = jnp.where(at_core == 1, enter, 0.0)
        one = v + pltpu.roll(jnp.where(lanes == 0, enter_p, v), 127, 1)
        one = one + pltpu.roll(jnp.where(lanes == 127, enter_m, v), 1, 1)
        two = one + pltpu.roll(jnp.where(lanes < 2, enter_p, v), 126, 1)
        two = two + pltpu.roll(jnp.where(lanes >= 126, enter_m, v), 2, 1)
        return one, two

    lane_t = lax.broadcasted_iota(jnp.int32, (nx + 16, 128), 1)
    core_t = jnp.full((nx + 16, 128), me_z, jnp.int32)
    for side in (0, 1):
        for r in (0, 1):
            one, two = along_z(trow[side, r], tyz[side, r], lane_t, core_t)
            zr[0, side, r] = one
            zr[1, side, r] = two

    low = pltpu.roll(tz[1], 128 - 2 * nx, 1)
    high = pltpu.roll(tz[2], 2 * nx, 1)
    columns = jnp.where(lane < 4, low, jnp.where(lane >= 2 * nx + 4, high, tz[0]))
    tz[0] = columns

    def slab_c(n, carry):
        at = jnp.clip(first_slab + n - 2, 0, px * nx - 1)
        wide = jnp.full((8, 128), radius[at], jnp.int32) == 2
        enter = pltpu.roll(tz[0], lax.rem(126 * me_z - 2 * n + 256, 128), 1)
        one, two = along_z(tp[n], enter, lane, core)
        v = jnp.where(wide, two, one)
        here = pl.ds(6 + n, 1)
        up_1 = jnp.where(wide, zr[1, 1, 0, here, :], zr[0, 1, 0, here, :])
        up_2 = zr[1, 1, 1, here, :]
        down_1 = jnp.where(wide, zr[1, 0, 1, here, :], zr[0, 0, 1, here, :])
        down_2 = zr[1, 0, 0, here, :]
        v_up = jnp.where(sub == 0, up_1, v)
        v_down = jnp.where(sub == 7, down_1, v)
        one = v + pltpu.roll(v_up, 7, 0) + pltpu.roll(v_down, 1, 0)
        two = one + pltpu.roll(jnp.where(sub == 1, up_2, v_up), 6, 0)
        two = two + pltpu.roll(jnp.where(sub == 6, down_2, v_down), 2, 0)
        Wb[0, n] = jnp.where(wide, two, one)
        Wb[1, n] = jnp.where(wide, two, 0.0)
        return carry

    lax.fori_loop(0, nx + 4, slab_c, 0, unroll=10)
    for x in range(nx):
        SE[x] = (Wb[0, x + 1] + Wb[0, x + 2]) + (Wb[0, x + 3] + (Wb[1, x] + Wb[1, x + 4]))
    last = pltpu.make_async_copy(SE, sens, out_sem.at[4])
    last.start()
    leave(ROUND_1, round_1)
    leave(ROUND_2, round_2)
    for store in stores:
        store.wait()
    last.wait()


def finish(pulled, solid, sens_in, out, sens):
    for x in range(solid.shape[0]):
        walls = solid[x] == 1
        p, mx, my, mz, h = (pulled[26 + k, x] for k in range(5))
        g = [pulled[i, x] for i in range(26)]
        out[0, x] = jnp.where(walls, g[0], -0.6 * g[0] + p)
        for i in range(1, 19, 2):
            cx, cy, cz = VECTORS[i]
            along = None
            for c, m in ((cx, mx), (cy, my), (cz, mz)):
                if c:
                    along = m if along is None else along + m if c > 0 else along - m
            out[i, x] = jnp.where(walls, g[i + 1], -0.6 * g[i] + (p + along))
            out[i + 1, x] = jnp.where(walls, g[i], -0.6 * g[i + 1] + (p - along))
        for i in range(19, 26):
            out[i, x] = -0.25 * g[i] + h
    sens[...] = sens_in[...]


def body(adjoint_state, macroscopic_state, design, solid, heated, face_labels, radius):
    count, nx, ny, nz = adjoint_state.shape
    assert (count, ny, nz) == (26, 8, 128) and lax.axis_size("gz") == 2 and nx == 16
    f32 = jnp.float32
    any_space = pl.BlockSpec(memory_space=pl.ANY)
    vmem = lambda *shape: pltpu.VMEM(shape, f32)
    dma = lambda n: pltpu.SemaphoreType.DMA((n,))

    def run(*refs):
        kernel(nx, *refs)

    pulled, sens = pl.pallas_call(
        run,
        out_shape=(
            jax.ShapeDtypeStruct((31,) + design.shape, f32),
            jax.ShapeDtypeStruct(design.shape, f32),
        ),
        in_specs=[any_space] * 6 + [pl.BlockSpec(memory_space=pltpu.SMEM)],
        out_specs=(any_space, any_space),
        scratch_shapes=[
            vmem(26, nx + 2, 8, 128),
            vmem(5, nx, 8, 128),
            vmem(nx, 8, 128),
            pltpu.VMEM((nx, 8, 128), jnp.int32),
            pltpu.VMEM((8, nx), jnp.int32),
            pltpu.VMEM((2, 8, 128), jnp.int32),
            vmem(31, nx, 8, 128),
            vmem(2, 6, 8, 128),
            vmem(2, 6, 8, 128),
            vmem(2, 6, nx, 128),
            vmem(2, 6, nx + 16, 128),
            vmem(8, 128),
            vmem(8, 128),
            vmem(2, 8, 128),
            vmem(2, nx, 128),
            vmem(nx + 4, 8, 128),
            vmem(2, 2, nx, 128),
            vmem(2, 2, nx + 16, 128),
            vmem(2, 2, nx + 16, 128),
            vmem(8, 128),
            vmem(3, 8, 128),
            vmem(2, 2, 2, nx + 16, 128),
            vmem(2, nx + 4, 8, 128),
            vmem(8, 128),
            vmem(nx, 8, 128),
            dma(6), dma(5),
            dma(len(ROUND_1)), dma(len(ROUND_1)),
            dma(len(ROUND_2)), dma(len(ROUND_2)),
        ],
        compiler_params=pltpu.CompilerParams(
            collective_id=0, has_side_effects=True, vmem_limit_bytes=56 * 1024 * 1024
        ),
    )(adjoint_state, macroscopic_state, design, solid, heated.T, face_labels, radius)
    step = 8
    cells = pl.BlockSpec((step, 8, 128), lambda n: (n, 0, 0))
    block = lambda count: pl.BlockSpec((count, step, 8, 128), lambda n: (0, n, 0, 0))
    return pl.pallas_call(
        finish,
        grid=(nx // step,),
        out_shape=(
            jax.ShapeDtypeStruct(adjoint_state.shape, f32),
            jax.ShapeDtypeStruct(design.shape, f32),
        ),
        in_specs=[block(31), cells, cells],
        out_specs=(block(26), cells),
        compiler_params=pltpu.CompilerParams(vmem_limit_bytes=56 * 1024 * 1024),
    )(pulled, solid, sens)


def solution(mesh):
    placed = (
        P(None, ("cases", "gx"), "gy", "gz"),
        P(None, ("cases", "gx"), "gy", "gz"),
        P(("cases", "gx"), "gy", "gz"),
        P(("cases", "gx"), "gy", "gz"),
        P(("cases", "gx"), "gy"),
        P("cases", "gy", "gz"),
        P("cases"),
    )
    return jax.shard_map(
        body,
        mesh=mesh,
        in_specs=placed,
        out_specs=(P(None, ("cases", "gx"), "gy", "gz"), P(("cases", "gx"), "gy", "gz")),
        check_vma=False,
    )
```

```python
import jax
import jax.numpy as jnp
from jax import lax
from jax.experimental import pallas as pl
from jax.experimental.pallas import tpu as pltpu
from jax.sharding import PartitionSpec as P

VECTORS = [
    (0, 0, 0),
    (1, 0, 0), (-1, 0, 0), (0, 1, 0), (0, -1, 0), (0, 0, 1), (0, 0, -1),
    (1, 1, 0), (-1, -1, 0), (1, -1, 0), (-1, 1, 0),
    (1, 0, 1), (-1, 0, -1), (1, 0, -1), (-1, 0, 1),
    (0, 1, 1), (0, -1, -1), (0, 1, -1), (0, -1, 1),
]
VECTORS = VECTORS + VECTORS[:7]
OPP = [0, 2, 1, 4, 3, 6, 5, 8, 7, 10, 9, 12, 11, 14, 13, 16, 15, 18, 17, 19, 21, 20, 23, 22, 25, 24]
X_FROM = ([2, 8, 10, 12, 14, 21], [1, 7, 9, 11, 13, 20])
Y_FROM = ([4, 8, 9, 16, 18, 23], [3, 7, 10, 15, 17, 22])
Z_PAIRS = [(5, 6, 0), (15, 17, 16), (18, 16, 32), (24, 25, 48), (11, 13, 64), (14, 12, 96)]
Z_BASE = {i: base for a, b, base in Z_PAIRS for i in (a, b)}
MESH = pl.DeviceIdType.MESH
W0, W1, W2 = 1.0 / 3.0, 1.0 / 18.0, 1.0 / 36.0

ROUND_1 = (
    [(dx, 0, 0) for dx in (1, -1)]
    + [(0, dy, 0) for dy in (1, -1)]
    + [(0, 0, 1)]
    + [(dx, dy, 0) for dx in (1, -1) for dy in (1, -1)]
    + [(dx, 0, 1) for dx in (1, -1)]
    + [(0, dy, 1) for dy in (1, -1)]
)
ROUND_1 = ROUND_1[5:] + ROUND_1[2:4] + ROUND_1[:2] + ROUND_1[4:5]
ROUND_2 = [(dx, dy, 1) for dx in (1, -1) for dy in (1, -1)] + ROUND_1


def kernel(
    nx, state, macro, design, solid, heated, faces, radius, out, sens,
    S, MA, DE, SO, HE, FA, O, xs, xr, ys, yh, zs, zh, xzr, yzr,
    tp, tys, trow, tyz, tzs, tz, zr, Wb, hT, SE,
    in_sem, out_sem, send1, recv1, send2, recv2,
):
    f32 = jnp.float32
    px, py = lax.axis_size("gx"), lax.axis_size("gy")
    me_c, me_x = lax.axis_index("cases"), lax.axis_index("gx")
    me_y, me_z = lax.axis_index("gy"), lax.axis_index("gz")

    def has(d):
        flag = None
        for delta, me, count in ((d[0], me_x, px), (d[1], me_y, py)):
            if delta == 0:
                continue
            here = me < count - 1 if delta > 0 else me > 0
            flag = here if flag is None else jnp.logical_and(flag, here)
        return flag

    def when(flag, body):
        if flag is None:
            body()
        else:
            pl.when(flag)(body)

    def target(d):
        return (me_c, me_x + d[0], me_y + d[1], 1 - me_z if d[2] else me_z)

    loads = [
        pltpu.make_async_copy(state, S.at[:, 1 : 1 + nx], in_sem.at[0]),
        pltpu.make_async_copy(macro, MA, in_sem.at[1]),
        pltpu.make_async_copy(design, DE, in_sem.at[2]),
        pltpu.make_async_copy(solid, SO, in_sem.at[3]),
        pltpu.make_async_copy(heated, HE, in_sem.at[4]),
        pltpu.make_async_copy(faces, FA, in_sem.at[5]),
    ]
    for load in loads:
        load.start()

    trow[...] = jnp.zeros_like(trow)
    tyz[...] = jnp.zeros_like(tyz)
    tz[...] = jnp.zeros_like(tz)
    tp[0:2] = jnp.zeros((2, 8, 128), f32)
    tp[nx + 2 : nx + 4] = jnp.zeros((2, 8, 128), f32)

    barrier = pltpu.get_barrier_semaphore()
    for d in ROUND_2:
        def greet(d=d):
            pl.semaphore_signal(barrier, inc=1, device_id=target(d), device_id_type=MESH)
        when(has(d), greet)

    lane = lax.broadcasted_iota(jnp.int32, (8, 128), 1)
    sub = lax.broadcasted_iota(jnp.int32, (8, 128), 0)
    edge = 127 * me_z
    mine = 127 - edge

    loads[0].wait()

    for side, (x_at, y_at) in enumerate(((nx, 7), (1, 0))):
        for j in range(6):
            xs[side, j] = S[X_FROM[side][j], x_at]
            ys[side, j] = S[Y_FROM[side][j], 1 : 1 + nx, y_at, :]

    def pack(x, acc):
        for first, second, base in Z_PAIRS:
            v = S[jnp.where(me_z == 1, first, second), x + 1]
            moved = pltpu.roll(v, lax.rem(base + x - mine + 256, 128), 1)
            acc = jnp.where(lane == base + x, moved, acc)
        return acc

    zs[...] = lax.fori_loop(0, nx, pack, jnp.zeros((8, 128), f32), unroll=True)

    beside_x = jnp.where(me_x > 0, 1, 0) + jnp.where(me_x < px - 1, 1, 0)
    beside_y = jnp.where(me_y > 0, 1, 0) + jnp.where(me_y < py - 1, 1, 0)
    pl.semaphore_wait(barrier, 2 * (beside_x + 1) * (beside_y + 1) - 1)

    def refs_1(d):
        dx, dy, dz = d
        side_x, side_y = (0 if dx > 0 else 1), (0 if dy > 0 else 1)
        if dx and dy:
            j = next(k for k, i in enumerate(Y_FROM[side_y]) if VECTORS[i][0] == -dx)
            if dx > 0:
                return ys.at[side_y, j, nx - 8 : nx], yh.at[side_y, j, 0:8]
            return ys.at[side_y, j, 0:8], yh.at[side_y, j, nx + 8 : nx + 16]
        if dx and dz:
            pair = (14, 12) if dx > 0 else (11, 13)
            return S.at[jnp.where(me_z == 1, pair[0], pair[1]), nx if dx > 0 else 1], xzr.at[side_x]
        if dy and dz:
            j = jnp.where(me_z == 1, 4, 3) if dy > 0 else jnp.where(me_z == 1, 3, 4)
            return ys.at[side_y, j], yzr.at[side_y]
        if dx:
            return xs.at[side_x], xr.at[side_x]
        if dy:
            return ys.at[side_y], yh.at[side_y, :, 8 : 8 + nx]
        return zs, zh

    def refs_2(d):
        dx, dy, dz = d
        side_y = 0 if dy > 0 else 1
        if dy:
            into = tyz if dz else trow
            if dx > 0:
                return tys.at[side_y, :, nx - 8 : nx], into.at[side_y, :, 0:8]
            if dx < 0:
                return tys.at[side_y, :, 0:8], into.at[side_y, :, nx + 8 : nx + 16]
            return tys.at[side_y], into.at[side_y, :, 8 : 8 + nx]
        if dz:
            return tzs, tz.at[0 if dx == 0 else 1 if dx > 0 else 2]
        if dx > 0:
            return tp.at[nx : nx + 2], tp.at[0:2]
        return tp.at[2:4], tp.at[nx + 2 : nx + 4]

    def copies(messages, refs, sends, recvs):
        made = []
        for n, d in enumerate(messages):
            src, dst = refs(d)
            made.append(
                pltpu.make_async_remote_copy(
                    src_ref=src, dst_ref=dst, send_sem=sends.at[n], recv_sem=recvs.at[n],
                    device_id=target(d), device_id_type=MESH,
                )
            )
        return made

    def start(messages, made):
        for d, copy in zip(messages, made):
            when(has(d), copy.start)

    def arrive(messages, made):
        for d, copy in zip(messages, made):
            when(has((-d[0], -d[1], d[2])), copy.wait_recv)

    def leave(messages, made):
        for d, copy in zip(messages, made):
            when(has(d), copy.wait_send)

    round_1 = copies(ROUND_1, refs_1, send1, recv1)
    start(ROUND_1, round_1)
    for load in loads[1:]:
        load.wait()

    hT[...] = jnp.zeros_like(hT)
    hT[:, 0:nx] = jnp.where(HE[...] == 1, 1.0, 0.0)

    core = jnp.full((8, 128), me_z, jnp.int32)
    col_p = (lane == 0) & (core == 0)
    col_m = (lane == 127) & (core == 1)
    out_z = {1: (lane == 127) & (core == 1), -1: (lane == 0) & (core == 0)}
    at_y = jnp.full((8, 128), me_y, jnp.int32)
    out_y = {1: (sub == 7) & (at_y == py - 1), -1: (sub == 0) & (at_y == 0)}
    face = {1: FA[1] == 1, -1: FA[0] == 1}
    heat_lane = (lane == 0) & (core == 0)

    arrive(ROUND_1, round_1)

    for side, at in ((0, 0), (1, nx + 1)):
        for j in range(6):
            S[X_FROM[side][j], at] = xr[side, j]
    lane_r = lax.broadcasted_iota(jnp.int32, (nx, 128), 1)
    core_r = jnp.full((nx, 128), me_z, jnp.int32)
    for side in (0, 1):
        for j in (3, 4):
            up = VECTORS[Y_FROM[side][j]][2] > 0
            mask = (lane_r == (0 if up else 127)) & (core_r == (0 if up else 1))
            yh[side, j, 8 : 8 + nx] = jnp.where(mask, yzr[side], yh[side, j, 8 : 8 + nx])
    cols = zh[...]
    cols = jnp.where(lane == 80, pltpu.roll(xzr[1], lax.rem(80 - edge + 128, 128), 1), cols)
    cols = jnp.where(lane == 95, pltpu.roll(xzr[0], lax.rem(95 - edge + 128, 128), 1), cols)
    zh[...] = cols

    first_slab = me_x * nx

    def slab_a(x, carry):
        cols = zh[...]
        at_x = jnp.full((8, 128), first_slab + x, jnp.int32)
        out_x = {1: at_x == px * nx - 1, -1: at_x == 0}
        column = {}
        for first, second, base in Z_PAIRS:
            k = base + x + VECTORS[first][0]
            column[base] = pltpu.roll(cols, lax.rem(edge - k + 256, 128), 1)
        g = []
        for i in range(26):
            cx, cy, cz = VECTORS[i]
            v = S[i, x + 1 + cx]
            if cz:
                v = jnp.where(col_p if cz > 0 else col_m, column[Z_BASE[i]], v)
            if cy:
                side = 0 if cy < 0 else 1
                row = yh[side, Y_FROM[side].index(i), pl.ds(8 + x + cx, 1), :]
                v = jnp.where(sub == (0 if cy > 0 else 7), row, v)
                v = pltpu.roll(v, 7 if cy > 0 else 1, 0)
            if cz:
                v = pltpu.roll(v, 127 if cz > 0 else 1, 1)
            if (cx, cy, cz) != (0, 0, 0):
                bounce = S[OPP[i], x + 1]
                leaves = None
                if cy:
                    leaves = out_y[cy]
                if cz:
                    leaves = out_z[cz] if leaves is None else leaves | out_z[cz]
                if cx:
                    opened = out_x[cx] & face[cx]
                    if leaves is not None:
                        opened = opened & jnp.logical_not(leaves)
                    bounce = jnp.where(opened, 0.0, bounce)
                    leaves = out_x[cx] if leaves is None else leaves | out_x[cx]
                v = jnp.where(leaves, bounce, v)
            O[i, x] = v
            g.append(v)
        s = {i: g[i] + g[i + 1] for i in range(1, 19, 2)}
        d = {i: g[i] - g[i + 1] for i in range(1, 19, 2)}
        xy, xz, yz = s[7] + s[9], s[11] + s[13], s[15] + s[17]
        g0 = W0 * g[0] + W1 * (s[1] + s[3] + s[5]) + W2 * (xy + xz + yz)
        g1x = W1 * d[1] + W2 * ((d[7] + d[9]) + (d[11] + d[13]))
        g1y = W1 * d[3] + W2 * ((d[7] - d[9]) + (d[15] + d[17]))
        g1z = W1 * d[5] + W2 * ((d[11] - d[13]) + (d[15] - d[17]))
        gxx = W1 * s[1] + W2 * (xy + xz)
        gyy = W1 * s[3] + W2 * (xy + yz)
        gzz = W1 * s[5] + W2 * (xz + yz)
        gxy, gxz, gyz = W2 * (s[7] - s[9]), W2 * (s[11] - s[13]), W2 * (s[15] - s[17])
        q0 = 0.25 * g[19] + 0.125 * ((g[20] + g[21]) + (g[22] + g[23]) + (g[24] + g[25]))
        q1x, q1y, q1z = (0.125 * (g[i] - g[i + 1]) for i in (20, 22, 24))
        rho, ux, uy, uz, temp = (MA[k, x] for k in range(5))
        fluid = jnp.where(SO[x] == 1, 0.0, 1.0)
        a = DE[x] * fluid
        aa = a * a
        tx = gxx * ux + gxy * uy + gxz * uz
        ty = gxy * ux + gyy * uy + gyz * uz
        tzz = gxz * ux + gyz * uy + gzz * uz
        quad = ux * tx + uy * ty + uz * tzz
        speed = ux * ux + uy * uy + uz * uz
        first_u = g1x * ux + g1y * uy + g1z * uz
        adv = q1x * ux + q1y * uy + q1z * uz
        both = 9.0 * quad - 3.0 * speed * g0
        buoy = 5.0 * a * temp / rho
        O[26, x] = 1.6 * (g0 - aa * (0.5 * both)) - buoy * adv
        O[27, x] = 1.6 * (3.0 * a * g1x + aa * (9.0 * tx - 3.0 * g0 * ux)) + buoy * q1x
        O[28, x] = 1.6 * (3.0 * a * g1y + aa * (9.0 * ty - 3.0 * g0 * uy)) + buoy * q1y
        O[29, x] = 1.6 * (3.0 * a * g1z + aa * (9.0 * tzz - 3.0 * g0 * uz)) + buoy * q1z
        hot = jnp.where(heat_lane, pltpu.roll(hT[...], lax.rem(128 - x, 128), 1), 0.0)
        O[30, x] = 1.25 * (q0 + 4.0 * a * adv) + 0.5 * hot
        term = fluid * (1.6 * rho * (3.0 * first_u + a * both) + 5.0 * temp * adv)
        reach = jnp.full((8, 128), radius[first_slab + x], jnp.int32)
        tp[x + 2] = term * jnp.where(reach == 2, 1.0 / 125.0, 1.0 / 27.0)
        return carry

    stores = []
    for n in range(4):
        lax.fori_loop(n * (nx // 4), (n + 1) * (nx // 4), slab_a, 0, unroll=4)
        part = pl.ds(n * (nx // 4), nx // 4)
        stores.append(pltpu.make_async_copy(O.at[:, part], out.at[:, part], out_sem.at[n]))
        stores[-1].start()

    for r in (0, 1):
        tys[0, r] = tp[2 : 2 + nx, 6 + r, :]
        tys[1, r] = tp[2 : 2 + nx, r, :]
    from_lane = 126 * (1 - me_z)
    packed = jnp.zeros((8, 128), f32)
    for x in range(nx):
        moved = pltpu.roll(tp[x + 2], lax.rem(2 * x + 4 - from_lane + 128, 128), 1)
        packed = jnp.where((lane >= 2 * x + 4) & (lane < 2 * x + 6), moved, packed)
    tzs[...] = packed

    round_2 = copies(ROUND_2, refs_2, send2, recv2)
    start(ROUND_2, round_2)

    arrive(ROUND_2, round_2)

    def along_z(v, enter, lanes, at_core):
        enter_p = jnp.where(at_core == 0, enter, 0.0)
        enter_m = jnp.where(at_core == 1, enter, 0.0)
        one = v + pltpu.roll(jnp.where(lanes == 0, enter_p, v), 127, 1)
        one = one + pltpu.roll(jnp.where(lanes == 127, enter_m, v), 1, 1)
        two = one + pltpu.roll(jnp.where(lanes < 2, enter_p, v), 126, 1)
        two = two + pltpu.roll(jnp.where(lanes >= 126, enter_m, v), 2, 1)
        return one, two

    lane_t = lax.broadcasted_iota(jnp.int32, (nx + 16, 128), 1)
    core_t = jnp.full((nx + 16, 128), me_z, jnp.int32)
    for side in (0, 1):
        for r in (0, 1):
            one, two = along_z(trow[side, r], tyz[side, r], lane_t, core_t)
            zr[0, side, r] = one
            zr[1, side, r] = two

    low = pltpu.roll(tz[1], 128 - 2 * nx, 1)
    high = pltpu.roll(tz[2], 2 * nx, 1)
    columns = jnp.where(lane < 4, low, jnp.where(lane >= 2 * nx + 4, high, tz[0]))
    tz[0] = columns

    def slab_c(n, carry):
        at = jnp.clip(first_slab + n - 2, 0, px * nx - 1)
        wide = jnp.full((8, 128), radius[at], jnp.int32) == 2
        enter = pltpu.roll(tz[0], lax.rem(126 * me_z - 2 * n + 256, 128), 1)
        one, two = along_z(tp[n], enter, lane, core)
        v = jnp.where(wide, two, one)
        here = pl.ds(6 + n, 1)
        up_1 = jnp.where(wide, zr[1, 1, 0, here, :], zr[0, 1, 0, here, :])
        up_2 = zr[1, 1, 1, here, :]
        down_1 = jnp.where(wide, zr[1, 0, 1, here, :], zr[0, 0, 1, here, :])
        down_2 = zr[1, 0, 0, here, :]
        v_up = jnp.where(sub == 0, up_1, v)
        v_down = jnp.where(sub == 7, down_1, v)
        one = v + pltpu.roll(v_up, 7, 0) + pltpu.roll(v_down, 1, 0)
        two = one + pltpu.roll(jnp.where(sub == 1, up_2, v_up), 6, 0)
        two = two + pltpu.roll(jnp.where(sub == 6, down_2, v_down), 2, 0)
        Wb[0, n] = jnp.where(wide, two, one)
        Wb[1, n] = jnp.where(wide, two, 0.0)
        return carry

    lax.fori_loop(0, nx + 4, slab_c, 0, unroll=True)
    for x in range(nx):
        SE[x] = (Wb[0, x + 1] + Wb[0, x + 2]) + (Wb[0, x + 3] + (Wb[1, x] + Wb[1, x + 4]))
    last = pltpu.make_async_copy(SE, sens, out_sem.at[4])
    last.start()
    leave(ROUND_1, round_1)
    leave(ROUND_2, round_2)
    for store in stores:
        store.wait()
    last.wait()


def finish(pulled, solid, sens_in, out, sens):
    for x in range(solid.shape[0]):
        walls = solid[x] == 1
        p, mx, my, mz, h = (pulled[26 + k, x] for k in range(5))
        g = [pulled[i, x] for i in range(26)]
        out[0, x] = jnp.where(walls, g[0], -0.6 * g[0] + p)
        for i in range(1, 19, 2):
            cx, cy, cz = VECTORS[i]
            along = None
            for c, m in ((cx, mx), (cy, my), (cz, mz)):
                if c:
                    along = m if along is None else along + m if c > 0 else along - m
            out[i, x] = jnp.where(walls, g[i + 1], -0.6 * g[i] + (p + along))
            out[i + 1, x] = jnp.where(walls, g[i], -0.6 * g[i + 1] + (p - along))
        for i in range(19, 26):
            out[i, x] = -0.25 * g[i] + h
    sens[...] = sens_in[...]


def body(adjoint_state, macroscopic_state, design, solid, heated, face_labels, radius):
    count, nx, ny, nz = adjoint_state.shape
    assert (count, ny, nz) == (26, 8, 128) and lax.axis_size("gz") == 2 and nx == 16
    f32 = jnp.float32
    any_space = pl.BlockSpec(memory_space=pl.ANY)
    vmem = lambda *shape: pltpu.VMEM(shape, f32)
    dma = lambda n: pltpu.SemaphoreType.DMA((n,))

    def run(*refs):
        kernel(nx, *refs)

    pulled, sens = pl.pallas_call(
        run,
        out_shape=(
            jax.ShapeDtypeStruct((31,) + design.shape, f32),
            jax.ShapeDtypeStruct(design.shape, f32),
        ),
        in_specs=[any_space] * 6 + [pl.BlockSpec(memory_space=pltpu.SMEM)],
        out_specs=(any_space, any_space),
        scratch_shapes=[
            vmem(26, nx + 2, 8, 128),
            vmem(5, nx, 8, 128),
            vmem(nx, 8, 128),
            pltpu.VMEM((nx, 8, 128), jnp.int32),
            pltpu.VMEM((8, nx), jnp.int32),
            pltpu.VMEM((2, 8, 128), jnp.int32),
            vmem(31, nx, 8, 128),
            vmem(2, 6, 8, 128),
            vmem(2, 6, 8, 128),
            vmem(2, 6, nx, 128),
            vmem(2, 6, nx + 16, 128),
            vmem(8, 128),
            vmem(8, 128),
            vmem(2, 8, 128),
            vmem(2, nx, 128),
            vmem(nx + 4, 8, 128),
            vmem(2, 2, nx, 128),
            vmem(2, 2, nx + 16, 128),
            vmem(2, 2, nx + 16, 128),
            vmem(8, 128),
            vmem(3, 8, 128),
            vmem(2, 2, 2, nx + 16, 128),
            vmem(2, nx + 4, 8, 128),
            vmem(8, 128),
            vmem(nx, 8, 128),
            dma(6), dma(5),
            dma(len(ROUND_1)), dma(len(ROUND_1)),
            dma(len(ROUND_2)), dma(len(ROUND_2)),
        ],
        compiler_params=pltpu.CompilerParams(
            collective_id=0, has_side_effects=True, vmem_limit_bytes=56 * 1024 * 1024
        ),
    )(adjoint_state, macroscopic_state, design, solid, heated.T, face_labels, radius)
    step = 8
    cells = pl.BlockSpec((step, 8, 128), lambda n: (n, 0, 0))
    block = lambda count: pl.BlockSpec((count, step, 8, 128), lambda n: (0, n, 0, 0))
    return pl.pallas_call(
        finish,
        grid=(nx // step,),
        out_shape=(
            jax.ShapeDtypeStruct(adjoint_state.shape, f32),
            jax.ShapeDtypeStruct(design.shape, f32),
        ),
        in_specs=[block(31), cells, cells],
        out_specs=(block(26), cells),
        compiler_params=pltpu.CompilerParams(vmem_limit_bytes=56 * 1024 * 1024),
    )(pulled, solid, sens)


def solution(mesh):
    placed = (
        P(None, ("cases", "gx"), "gy", "gz"),
        P(None, ("cases", "gx"), "gy", "gz"),
        P(("cases", "gx"), "gy", "gz"),
        P(("cases", "gx"), "gy", "gz"),
        P(("cases", "gx"), "gy"),
        P("cases", "gy", "gz"),
        P("cases"),
    )
    return jax.shard_map(
        body,
        mesh=mesh,
        in_specs=placed,
        out_specs=(P(None, ("cases", "gx"), "gy", "gz"), P(("cases", "gx"), "gy", "gz")),
        check_vma=False,
    )
```
